512 devices in a mesh: sx: 16 (over z, core), sy: 4 (over x), mom: 8 (over y).
Axes of the slice: x: 4, y: 8, z: 8, core: 2. Of those that a mesh axis runs over, the one named last changes fastest.
Arguments:
- propagator: bfloat16 [2, 12, 12, 64, 6144], P(None, None, None, 'sx', 'sy'), may hold values from -2.6875 to 2.6875
- momenta: int32 [128, 3], P('mom'), may hold values from -4 to 4
- chan_moms: int32 [16, 2], replicated, may hold values from 0 to 127
- term_index: int32 [2, 16, 1536], P(None, 'mom', ('sx', 'sy')), may hold values from 0 to 1727
- term_weight: float32 [16, 1536], P('mom', ('sx', 'sy')), may hold values from -0.24 to 0.24
- lengths: int32 [16], P('mom'), may hold values from 1 to 1536, 8192 in all
Outputs:
- projected: float32 [128, 3456], P('mom', ('sx', 'sy'))
- correlator: float32 [2, 16], P(None, 'mom')
The draws below stay inside these ranges and needn't reach their ends.
Inputs may be any that keep to these rules, and one draw needn't show every extreme that they name: The lengths of all 16 channels sum to 8192; the longest list has exactly 1536 live terms.
All inputs are finite; a program needn't handle non-finite values. No bound on the sum of `lengths` on one device may be relied on, other than what follows from the above.
Results may differ from the reference program's by a relative error of at most 0.0058.
Values sent between devices are 32-bit elements; how exact they have to be, the bound alone decides.
A program may use at most 64 MiB of HBM per device.

```python
import math
import jax
import jax.numpy as jnp
import numpy as np
from jax import lax

LAT = 96
NMOM = 128
NX = 64
NY = 64
NCH = 16
LMAX = 1536
LMEAN = 512


def plant(result, rng, least, top_value):
    longest = result.shape.index(max(result.shape))
    spots = []
    for shift in (0, 1):
        where = [jax.random.randint(jax.random.fold_in(rng, axis), (), 0, length) for axis, length in enumerate(result.shape)]
        where[longest] = (where[longest] + shift) % result.shape[longest]
        spots.append(tuple(where))
    return result.at[spots[0]].set(least).at[spots[1]].set(top_value)


def block_scale(own_key, extent, shards, smallest, top_value):
    def one(position, blocks):
        steps = jax.random.uniform(jax.random.fold_in(jax.random.fold_in(own_key, 6), position), (blocks,), jnp.float32, smallest / len(shards), top_value / len(shards))
        return jnp.repeat(jnp.exp(steps), extent[position] // blocks).reshape((-1,) + (1,) * (len(extent) - position - 1))

    factor_of = one(*shards[0])
    for cut in shards[1:]:
        factor_of = factor_of * one(*cut)
    return factor_of


def split_up(count, total, bound, slope):
    loads = [(1 << 20) // math.isqrt(rank ** slope) + 1 for rank in range(2, count + 1)]
    spare, counts = total - bound - (count - 1), [1] * (count - 1)
    while spare > 0:
        movable = [i for i in range(count - 1) if counts[i] < bound]
        pool, left = sum([loads[i] for i in movable]), spare
        for i in movable:
            extra = min(bound - counts[i], max(1, left * loads[i] // pool), spare)
            counts[i] = counts[i] + extra
            spare = spare - extra
    return np.array([bound] + counts)


def ragged_sizes(own_key, amount, total, bound, skew):
    if amount == 2:
        one = jax.random.randint(own_key, (), max(1, total - bound), min(bound, total - 1) + 1)
        return jnp.stack([one, total - one])
    sizes = jnp.asarray(split_up(amount, total, bound, skew), jnp.int32)
    twos = (amount - 1) // 2
    donor, sink = sizes[1:1 + 2 * twos:2], sizes[2:2 + 2 * twos:2]
    room = jnp.minimum(donor - 1, bound - sink)
    moved = jax.random.randint(jax.random.fold_in(own_key, 1), (twos,), 0, 1 << 20) % (room + 1)
    sizes = sizes.at[1:1 + 2 * twos:2].set(donor - moved).at[2:2 + 2 * twos:2].set(sink + moved)
    return sizes[jax.random.permutation(jax.random.fold_in(own_key, 2), amount)]


def noise(key, dims, width, limit, pieces=(), kind=jnp.bfloat16):
    level = block_scale(key, dims, pieces, -0.22, 0.18) if pieces else 1.0
    drawn = jax.random.normal(key, dims, jnp.float32) * width * level
    return jnp.minimum(jnp.maximum(drawn, -limit), limit).astype(kind)


def setup_inputs(seed: int = 0) -> dict:
    seeds = jax.random.split(jax.random.key(seed), 7)
    return {
        "propagator": noise(seeds[0], (2, 12, 12, NX, NY * LAT), 0.45, 2.6875, ((3, 16), (4, 4))),
        "momenta": plant(jax.random.randint(seeds[1], (NMOM, 3), -4, 5), jax.random.fold_in(seeds[1], 1), -4, 4).astype(jnp.int32),
        "chan_moms": plant(jax.random.randint(seeds[2], (NCH, 2), 0, NMOM), jax.random.fold_in(seeds[2], 1), 0, NMOM - 1).astype(jnp.int32),
        "term_index": plant(jax.random.randint(seeds[3], (2, NCH, LMAX), 0, 1728), jax.random.fold_in(seeds[3], 1), 0, 1727).astype(jnp.int32),
        "term_weight": noise(seeds[4], (NCH, LMAX), 0.04, 0.24, ((0, 8), (1, 64)), jnp.float32),
        "lengths": ragged_sizes(seeds[5], NCH, NCH * LMEAN, LMAX, 2).astype(jnp.int32),
    }


SPIN_SIGN = (-1.0, 1.0, -1.0, 1.0)
SPIN_FROM = (1, 0, 3, 2)
COLOUR_PAIRS = ((1, 2, 0), (2, 0, 1), (0, 1, 2))

def diquark_pairs(lift_real, lift_imag, prop_real, prop_imag, left_colour, right_colour):
    site_count = prop_real.shape[-1]
    total_real = jnp.zeros((12, 12, site_count), jnp.float32)
    total_imag = jnp.zeros((12, 12, site_count), jnp.float32)
    for spin_index in range(4):
        left_real = lift_real[left_colour, spin_index][:, None, :]
        left_imag = lift_imag[left_colour, spin_index][:, None, :]
        right_real = prop_real[right_colour, spin_index][None, :, :]
        right_imag = prop_imag[right_colour, spin_index][None, :, :]
        total_real = total_real + left_real * right_real - left_imag * right_imag
        total_imag = total_imag + left_real * right_imag + left_imag * right_real
    return (total_real, total_imag)

def baryon_block(site_values):
    site_count = site_values.shape[-1]
    prop_real = site_values[0].reshape(3, 4, 12, site_count)
    prop_imag = site_values[1].reshape(3, 4, 12, site_count)
    lift_real = jnp.stack([SPIN_SIGN[spin_index] * prop_real[:, SPIN_FROM[spin_index]] for spin_index in range(4)], axis=1)
    lift_imag = jnp.stack([SPIN_SIGN[spin_index] * prop_imag[:, SPIN_FROM[spin_index]] for spin_index in range(4)], axis=1)
    block_real = jnp.zeros((12, 12, 12, site_count), jnp.float32)
    block_imag = jnp.zeros((12, 12, 12, site_count), jnp.float32)
    for left_colour, right_colour, third_colour in COLOUR_PAIRS:
        plus_real, plus_imag = diquark_pairs(lift_real, lift_imag, prop_real, prop_imag, left_colour, right_colour)
        minus_real, minus_imag = diquark_pairs(lift_real, lift_imag, prop_real, prop_imag, right_colour, left_colour)
        diquark_real = (plus_real - minus_real)[:, :, None, :]
        diquark_imag = (plus_imag - minus_imag)[:, :, None, :]
        quark_real = prop_real[third_colour, 0][None, None, :, :]
        quark_imag = prop_imag[third_colour, 0][None, None, :, :]
        block_real = block_real + diquark_real * quark_real - diquark_imag * quark_imag
        block_imag = block_imag + diquark_real * quark_imag + diquark_imag * quark_real
    joined = jnp.concatenate([block_real.reshape(1728, site_count), block_imag.reshape(1728, site_count)], axis=0)
    return joined.astype(jnp.bfloat16)

def phase_rows(momenta, coord_x, coord_y, coord_z):
    turns = (momenta[:, 0:1] * coord_x[None, :] + momenta[:, 1:2] * coord_y[None, :] + momenta[:, 2:3] * coord_z[None, :]) % LAT
    angle = turns.astype(jnp.float32) * (2.0 * math.pi / LAT)
    return jnp.concatenate([jnp.cos(angle), jnp.sin(angle)], axis=0).astype(jnp.bfloat16)

def combine_parts(accumulated, mom_rows):
    half_width = accumulated.shape[1] // 2
    top_rows = accumulated[:mom_rows]
    bottom_rows = accumulated[mom_rows:]
    return jnp.concatenate([top_rows[:, :half_width] + bottom_rows[:, half_width:], top_rows[:, half_width:] - bottom_rows[:, :half_width]], axis=1)

def correlate(first_rows, second_rows, left_index, right_index, live_weight):
    half_width = first_rows.shape[1] // 2
    left_real = jnp.take_along_axis(first_rows, left_index, axis=1)
    left_imag = jnp.take_along_axis(first_rows, left_index + half_width, axis=1)
    right_real = jnp.take_along_axis(second_rows, right_index, axis=1)
    right_imag = jnp.take_along_axis(second_rows, right_index + half_width, axis=1)
    corr_real = lax.optimization_barrier(jnp.sum(live_weight * (left_real * right_real - left_imag * right_imag), axis=1))
    corr_imag = lax.optimization_barrier(jnp.sum(live_weight * (left_real * right_imag + left_imag * right_real), axis=1))
    return jnp.stack([corr_real, corr_imag], axis=0)

def reference(propagator, momenta, chan_moms, term_index, term_weight, lengths):
    row_sites = NY * LAT
    local_site = jnp.arange(row_sites, dtype=jnp.int32)

    def add_row(running_sum, row_index):
        site_values = lax.dynamic_index_in_dim(propagator, row_index, 3, keepdims=False).astype(jnp.float32)
        block_values = baryon_block(site_values).astype(jnp.float32)
        coord_x = jnp.zeros((row_sites,), jnp.int32) + row_index
        phases = phase_rows(momenta, coord_x, local_site // LAT, local_site % LAT).astype(jnp.float32)
        product = lax.dot_general(phases, block_values, (((1,), (1,)), ((), ())), precision=lax.Precision.HIGHEST, preferred_element_type=jnp.float32)
        return (running_sum + product, None)
    initial = jnp.zeros((2 * NMOM, 3456), jnp.float32)
    accumulated, unused = lax.scan(add_row, initial, jnp.arange(NX, dtype=jnp.int32))
    projected = combine_parts(accumulated, NMOM) * (1.0 / math.sqrt(NX * NY * LAT))
    slot_index = jnp.arange(LMAX, dtype=jnp.int32)
    live_weight = jnp.where(slot_index[None, :] < lengths[:, None], term_weight, 0.0)
    correlator = correlate(projected[chan_moms[:, 0]], projected[chan_moms[:, 1]], term_index[0], term_index[1], live_weight)
    return (projected, correlator)
```

```python
import math
import jax
import jax.numpy as jnp
from jax import lax
from jax.experimental import pallas as pl
from jax.experimental.pallas import tpu as pltpu
from jax.sharding import PartitionSpec as P

LAT = 96
PAIRS = 10
SCALE = 1.0 / math.sqrt(393216)
COLOURS = ((1, 2, 0), (2, 0, 1), (0, 1, 2))


def sine(turns):
    u = turns - 96.0 * jnp.floor(turns * (1.0 / 96.0) + 0.5)
    v = jnp.where(u > 24.0, 48.0 - u, jnp.where(u < -24.0, -48.0 - u, u))
    x = v * (2.0 * math.pi / 96.0)
    y = x * x
    r = jnp.float32(1.0 / 6227020800.0)
    for c in (-1.0 / 39916800.0, 1.0 / 362880.0, -1.0 / 5040.0, 1.0 / 120.0, -1.0 / 6.0, 1.0):
        r = r * y + c
    return x * r


def cosine(turns):
    return sine(turns + 24.0)


def cmul(a, b):
    return (a[0] * b[0] - a[1] * b[1], a[0] * b[1] + a[1] * b[0])


def cadd(a, b):
    return (a[0] + b[0], a[1] + b[1])


def csub(a, b):
    return (a[0] - b[0], a[1] - b[1])


def start_loads(s_hbm, buf, sem):
    for t in range(3):
        for c in range(4 * t, 4 * t + 4):
            pltpu.make_async_copy(
                s_hbm.at[:, :, :, :, pl.ds(128 * c, 128)], buf.at[:, :, :, c], sem.at[t]
            ).start()


def wait_load(buf, sem, t):
    part = buf.at[:, :, :, 4 * t : 4 * t + 4]
    pltpu.make_async_copy(part, part, sem.at[t]).wait()


def fill_phases(mom, rhs, tab):
    x3 = lax.broadcasted_iota(jnp.int32, (96, 128), 0).astype(jnp.float32)
    c3 = cosine(mom[2:3] * x3)
    s3 = sine(mom[2:3] * x3)
    x2 = lax.broadcasted_iota(jnp.int32, (16, 128), 0).astype(jnp.float32)
    tab[0] = cosine(mom[1:2] * x2)
    tab[1] = sine(mom[1:2] * x2)

    def row(b, _):
        c2 = tab[0, pl.ds(b, 1), :]
        s2 = tab[1, pl.ds(b, 1), :]
        at = pl.ds(pl.multiple_of(96 * b, 96), 96)
        rhs[at, 0:128] = (c2 * c3 - s2 * s3).astype(jnp.bfloat16)
        rhs[at, 128:256] = (s2 * c3 + c2 * s3).astype(jnp.bfloat16)
        return 0

    lax.fori_loop(0, 16, row, 0)


def blocks(t, y, buf, sem, skp, lhs):
    low = lax.broadcasted_iota(jnp.int32, (8, 128), 0) < 4

    def rot(v):
        return pltpu.roll(v, 4, 0)

    def load(part, row, i):
        return buf[part, row, i, 4 * t : 4 * t + 4].reshape(16, 128).astype(jnp.float32)

    def pack_k(kp, _):
        for part in range(2):
            for c in range(3):
                a = load(part, 4 * c, 2 * kp)
                b = load(part, 4 * c, 2 * kp + 1)
                for h in range(2):
                    ah, bh = a[8 * h : 8 * h + 8], b[8 * h : 8 * h + 8]
                    skp[2 * h, part, c, kp] = jnp.where(low, ah, rot(bh))
                    skp[2 * h + 1, part, c, kp] = jnp.where(low, rot(ah), bh)
        return 0

    def spins(colour, idx):
        return [(load(0, 4 * colour + s, idx), load(1, 4 * colour + s, idx)) for s in range(4)]

    def pair(p, _):
        e = PAIRS * y + p
        d = e // 12
        i = e - 12 * d
        j = lax.rem(i + d, 12)
        q = []
        for a, b, c in COLOURS:
            A, B, A2, B2 = spins(a, i), spins(b, j), spins(a, j), spins(b, i)
            total = None
            for s, u in ((0, 1), (2, 3)):
                term = csub(cmul(A[s], B[u]), cmul(A[u], B[s]))
                term = cadd(term, csub(cmul(A2[s], B2[u]), cmul(A2[u], B2[s])))
                total = term if total is None else cadd(total, term)
            q.append((c, total))
        for ch in range(4):
            h, odd = ch // 2, ch % 2
            dup = {}
            for c, total in q:
                both = []
                for v in total:
                    v = v[8 * h : 8 * h + 8]
                    r = rot(v)
                    both.append(jnp.where(low, r, v) if odd else jnp.where(low, v, r))
                dup[c] = tuple(both)
            for kq in range(3):
                halves = []
                for kp in (2 * kq, 2 * kq + 1):
                    tot = None
                    for c in range(3):
                        prod = cmul(dup[c], (skp[ch, 0, c, kp], skp[ch, 1, c, kp]))
                        tot = prod if tot is None else cadd(tot, prod)
                    halves.append(tot)
                for part in range(2):
                    rows = pl.ds(pl.multiple_of(96 * p + 48 * part + 16 * kq, 16), 16)
                    lanes = slice(512 * t + 128 * ch, 512 * t + 128 * ch + 128)
                    lhs[rows, lanes] = jnp.concatenate(
                        [halves[0][part], halves[1][part]], axis=0
                    ).astype(jnp.bfloat16)
        return 0

    wait_load(buf, sem, t)
    lax.fori_loop(0, 6, pack_k, 0)
    lax.fori_loop(0, PAIRS, pair, 0)


def finish(mom, x0, y0, scale, chan, acc, zbuf, part1):
    x1 = lax.broadcasted_iota(jnp.int32, (8, 128), 0) % 4 + x0
    turns = mom[0:1] * x1.astype(jnp.float32) + mom[1:2] * y0.astype(jnp.float32)
    fc, fs = cosine(turns) * scale, sine(turns) * scale

    def pair(p, _):
        for g in range(6):
            r = acc[pl.ds(pl.multiple_of(96 * p + 8 * g, 8), 8), :]
            m = acc[pl.ds(pl.multiple_of(96 * p + 48 + 8 * g, 8), 8), :]
            re = r[:, :128] + m[:, 128:]
            im = m[:, :128] - r[:, 128:]
            at = pl.ds(pl.multiple_of(48 * p + 8 * g, 8), 8)
            zbuf[0, at, :] = fc * re + fs * im
            zbuf[1, at, :] = fc * im - fs * re
        return 0

    lax.fori_loop(0, PAIRS, pair, 0)
    zbuf[:, 480:512, :] = jnp.zeros((2, 32, 128), jnp.float32)
    for part in range(2):
        tot = zbuf[part, pl.ds(0, 128, stride=4), :]
        for k in range(1, 4):
            tot = tot + zbuf[part, pl.ds(k, 128, stride=4), :]
        turned = tot.T
        for g in range(8):
            part1[g, 16 * part : 16 * part + 16, :] = turned[16 * g : 16 * g + 16]
    for g in range(8):
        for k in range(4):
            n = chan[2 * g + k // 2, k % 2]
            for part in range(2):
                row = part1[pl.ds(n // 16, 1), pl.ds(16 * part + n % 16, 1), :]
                at = 32 + 2 * k + part
                part1[g : g + 1, at : at + 1, :] = row


def place(m):
    i = jnp.floor((m + 0.5) * (1.0 / 144.0))
    r = m - 144.0 * i
    j = jnp.floor((r + 0.5) * (1.0 / 12.0))
    k = r - 12.0 * j
    d = j - i
    d = jnp.where(d < 0.0, d + 12.0, d)
    flip = (d > 6.0) | ((d == 6.0) & (i >= 6.0))
    e = jnp.where(flip, 12.0 * (12.0 - d) + j, 12.0 * d + i)
    slot = jnp.floor((e + 0.5) * (1.0 / PAIRS))
    return slot, (e - PAIRS * slot) * 12.0 + k


def pick(x, lane):
    return jnp.take_along_axis(x, lane, axis=1, mode="promise_in_bounds")


def kernel(
    s_hbm, momenta, chan, tindex, tweight, lengths, out, corr,
    buf, rhs, tab, skp, lhs, acc, zbuf,
    mom_box, term_box, term_all, part1, got1, part2, got2, part3, got3,
    chan4, rows4, gotc, goto, load_sem, send_sem, recv_sem,
):
    sx, x, y = lax.axis_index("sx"), lax.axis_index("sy"), lax.axis_index("mom")
    z, core = sx // 2, lax.rem(sx, 2)
    b = 4 * core + x

    def b_dev(g):
        return (2 * z + g // 4, lax.rem(g, 4), y)

    def z_dev(g):
        return (2 * g + core, x, y)

    def y_dev(g):
        return (sx, x, g)

    def step(v, o):
        return lax.rem(v + o, 8)

    def copy(src, dst, stage, o, dev):
        return pltpu.make_async_remote_copy(
            src_ref=src, dst_ref=dst, send_sem=send_sem.at[stage, o],
            recv_sem=recv_sem.at[stage, o], device_id=dev,
            device_id_type=pl.DeviceIdType.MESH,
        )

    start_loads(s_hbm, buf, load_sem)
    barrier = pltpu.get_barrier_semaphore()
    for o in range(1, 8):
        for dev in (b_dev(step(b, o)), z_dev(step(z, o)), y_dev(step(y, o))):
            pl.semaphore_signal(
                barrier, inc=1, device_id=dev, device_id_type=pl.DeviceIdType.MESH
            )
        pl.semaphore_signal(
            barrier, inc=1, device_id=(2 * z + y // 4, lax.rem(y, 4), step(y, o)),
            device_id_type=pl.DeviceIdType.MESH,
        )
    alone = b == y

    @pl.when(jnp.logical_not(alone))
    def _():
        pl.semaphore_signal(
            barrier, inc=1, device_id=(2 * z + y // 4, lax.rem(y, 4), y),
            device_id_type=pl.DeviceIdType.MESH,
        )

    blocks(0, y, buf, load_sem, skp, lhs)

    rows = lax.broadcasted_iota(jnp.int32, (8, 128), 0)
    lanes = lax.broadcasted_iota(jnp.int32, (8, 128), 1)
    tile = jnp.zeros((8, 128), jnp.float32)
    for n in range(16):
        here = lanes == 16 * y + n
        for k in range(3):
            tile = jnp.where(here & (rows == k), momenta[n, k].astype(jnp.float32), tile)
    mom_box[0] = tile

    term_box[0] = jnp.zeros((8, 128), jnp.float32)
    live = lax.broadcasted_iota(jnp.int32, (2, 24), 1) + (8 * z + b) * 24
    owner = lax.broadcasted_iota(jnp.int32, (2, 24), 0)
    size = jnp.where(owner == 0, lengths[0], lengths[1])
    for side in range(2):
        slot, lane = place(tindex[side].astype(jnp.float32))
        term_box[0, 2 * side : 2 * side + 2, 0:24] = slot * 128.0 + lane
    term_box[0, 4:6, 0:24] = jnp.where(live < size, tweight[...], 0.0)
    term_box[0] = pltpu.roll(term_box[0], 32 * lax.rem(b, 4), 1)

    pl.semaphore_wait(barrier, jnp.where(alone, 28, 29))
    sent = []
    for o in range(1, 8):
        c = copy(mom_box.at[0], mom_box.at[o], 0, o, y_dev(step(y, o)))
        c.start()
        sent.append(c)
    boxes = []
    for o in range(1, 8):
        c = copy(term_box.at[0], term_box.at[o], 1, o, b_dev(step(b, o)))
        c.start()
        boxes.append(c)

    blocks(1, y, buf, load_sem, skp, lhs)

    for c in sent:
        c.wait_recv()
    mom = mom_box[0]
    for o in range(1, 8):
        mom = mom + mom_box[o]
    for c in boxes:
        c.wait_recv()
    for half in range(2):
        joined = jnp.zeros((8, 128), jnp.float32)
        for o in range(8):
            source = lax.rem(b + 8 - o, 8)
            joined = joined + jnp.where(source // 4 == half, term_box[o], 0.0)
        term_all[z, half] = joined
    sent += boxes
    boxes = []
    for o in range(1, 8):
        c = copy(term_all.at[z], term_all.at[z], 2, o, z_dev(step(z, o)))
        c.start()
        boxes.append(c)

    blocks(2, y, buf, load_sem, skp, lhs)
    fill_phases(mom, rhs, tab)
    acc[...] = jnp.dot(lhs[...], rhs[...], preferred_element_type=jnp.float32)
    finish(mom, 4 * sx, 16 * x, SCALE, chan, acc, zbuf, part1)

    hops = []
    for o in range(1, 8):
        g = step(b, o)
        c = copy(part1.at[g], got1.at[o], 3, o, b_dev(g))
        c.start()
        hops.append(c)
    total = part1[b]
    for c in hops:
        c.wait_recv()
    for o in range(1, 8):
        total = total + got1[o]
    sent += hops
    got1[0] = total
    for g in range(8):
        part2[g, 0:2] = got1[0, 2 * g : 2 * g + 2]
        part2[g, 2:4] = got1[0, 16 + 2 * g : 18 + 2 * g]
        part2[g, 4:5] = got1[0, 32 + g : 33 + g]
        part2[g, 5:8] = jnp.zeros((3, 128), jnp.float32)

    hops = []
    for o in range(1, 8):
        g = step(z, o)
        c = copy(part2.at[g], got2.at[o], 4, o, z_dev(g))
        c.start()
        hops.append(c)
    total = part2[z]
    for c in hops:
        c.wait_recv()
    for o in range(1, 8):
        total = total + got2[o]
    sent += hops
    part3[...] = total

    def third(o, slot):
        g = step(b, o)
        return pltpu.make_async_remote_copy(
            src_ref=part3, dst_ref=got3.at[slot], send_sem=send_sem.at[5, o],
            recv_sem=recv_sem.at[5, slot], device_id=(2 * z + g // 4, lax.rem(g, 4), b),
            device_id_type=pl.DeviceIdType.MESH,
        )

    for o in range(1, 8):
        third(o, y).start()

    @pl.when(jnp.logical_not(alone))
    def _():
        third(0, y).start()

    @pl.when(alone)
    def _():
        got3[y] = part3[...]

    for k in range(8):
        @pl.when(jnp.logical_not(alone & (y == k)))
        def _():
            third(0, k).wait_recv()

    column = (lanes + 54 * (8 * lax.rem(rows, 4) + b)).astype(jnp.float32)
    slot, lane = place(column)
    lane = lane.astype(jnp.int32)
    first = rows < 4
    news = [jnp.zeros((8, 128), jnp.float32), jnp.zeros((8, 128), jnp.float32)]
    for k in range(8):
        have = got3[k]
        for n in range(2):
            real = jnp.broadcast_to(have[n : n + 1], (8, 128))
            imag = jnp.broadcast_to(have[n + 2 : n + 3], (8, 128))
            value = pick(jnp.where(first, real, imag), lane)
            news[n] = jnp.where(slot == k, value, news[n])
    for g in range(8):
        for n in range(2):
            rows4[g, n : n + 1] = news[n][g : g + 1]
    chan4[...] = got3[:, 4, :]
    gotc[z] = chan4[...]
    goto[z] = rows4[z]

    hops = []
    for o in range(1, 8):
        g = step(z, o)
        c = copy(chan4, gotc.at[z], 6, o, z_dev(g))
        c.start()
        hops.append(c)
        c = copy(rows4.at[g], goto.at[z], 7, o, z_dev(g))
        c.start()
        hops.append(c)
    for c in boxes:
        c.wait_recv()
    sent += boxes
    terms = [term_all[:, :, k, :].reshape(16, 128) for k in range(6)]
    for c in hops:
        c.wait_recv()
    sent += hops
    answer = jnp.zeros((2, 2), jnp.float32)
    at_row = lax.broadcasted_iota(jnp.int32, (2, 2), 0)
    at_col = lax.broadcasted_iota(jnp.int32, (2, 2), 1)
    for h in range(2):
        sides = []
        for side in range(2):
            slot = jnp.floor((terms[2 * side + h] + 0.5) * (1.0 / 128.0))
            lane = (terms[2 * side + h] - 128.0 * slot).astype(jnp.int32)
            both = []
            for part in range(2):
                table = gotc[4 * h + 2 * side + part]
                chosen = []
                for u in range(2):
                    value = jnp.zeros((8, 128), jnp.float32)
                    for k in range(8):
                        have = pick(
                            jnp.broadcast_to(table[k : k + 1], (8, 128)), lane[8 * u : 8 * u + 8]
                        )
                        value = jnp.where(slot[8 * u : 8 * u + 8] == k, have, value)
                    chosen.append(value)
                both.append(jnp.concatenate(chosen, axis=0))
            sides.append(tuple(both))
        prod = cmul(sides[0], sides[1])
        for part in range(2):
            answer = jnp.where(
                (at_row == part) & (at_col == h), jnp.sum(terms[4 + h] * prod[part]), answer
            )
    corr[...] = answer
    out[...] = goto[...].reshape(16, 128)[:, :54]

    for c in sent:
        c.wait_send()
    for o in range(1, 8):
        third(o, y).wait_send()

    @pl.when(jnp.logical_not(alone))
    def _():
        third(0, y).wait_send()


def local(propagator, momenta, chan_moms, term_index, term_weight, lengths):
    f32 = jnp.float32
    vmem = pl.BlockSpec(memory_space=pltpu.VMEM)
    smem = pl.BlockSpec(memory_space=pltpu.SMEM)
    return pl.pallas_call(
        kernel,
        out_shape=(
            jax.ShapeDtypeStruct((16, 54), f32),
            jax.ShapeDtypeStruct((2, 2), f32),
        ),
        in_specs=[pl.BlockSpec(memory_space=pl.ANY), smem, smem, vmem, vmem, smem],
        out_specs=(vmem, vmem),
        scratch_shapes=[
            pltpu.VMEM((2, 12, 12, 12, 4, 128), jnp.bfloat16),
            pltpu.VMEM((1536, 256), jnp.bfloat16),
            pltpu.VMEM((2, 16, 128), f32),
            pltpu.VMEM((4, 2, 3, 6, 8, 128), f32),
            pltpu.VMEM((96 * PAIRS, 1536), jnp.bfloat16),
            pltpu.VMEM((96 * PAIRS, 256), f32),
            pltpu.VMEM((2, 512, 128), f32),
            pltpu.VMEM((8, 8, 128), f32),
            pltpu.VMEM((8, 8, 128), f32),
            pltpu.VMEM((8, 2, 8, 128), f32),
            pltpu.VMEM((8, 40, 128), f32),
            pltpu.VMEM((8, 40, 128), f32),
            pltpu.VMEM((8, 8, 128), f32),
            pltpu.VMEM((8, 8, 128), f32),
            pltpu.VMEM((8, 128), f32),
            pltpu.VMEM((8, 8, 128), f32),
            pltpu.VMEM((8, 128), f32),
            pltpu.VMEM((8, 2, 128), f32),
            pltpu.VMEM((8, 8, 128), f32),
            pltpu.VMEM((8, 2, 128), f32),
            pltpu.SemaphoreType.DMA((3,)),
            pltpu.SemaphoreType.DMA((8, 8)),
            pltpu.SemaphoreType.DMA((8, 8)),
        ],
        compiler_params=pltpu.CompilerParams(
            collective_id=0, has_side_effects=True, vmem_limit_bytes=40 * 2**20
        ),
    )(propagator, momenta, chan_moms, term_index, term_weight, lengths)


def solution(mesh):
    in_specs = (
        P(None, None, None, "sx", "sy"),
        P("mom", None),
        P(),
        P(None, "mom", ("sx", "sy")),
        P("mom", ("sx", "sy")),
        P("mom"),
    )
    out_specs = (P("mom", ("sx", "sy")), P(None, "mom"))
    return jax.shard_map(local, mesh=mesh, in_specs=in_specs, out_specs=out_specs, check_vma=False)
```

```python
import math
import jax
import jax.numpy as jnp
from jax import lax
from jax.experimental import pallas as pl
from jax.experimental.pallas import tpu as pltpu
from jax.sharding import PartitionSpec as P

LAT = 96
PAIRS = 10
SCALE = 1.0 / math.sqrt(393216)
IM = 24
COLOURS = ((1, 2, 0), (2, 0, 1), (0, 1, 2))


def sine(turns):
    u = turns - 96.0 * jnp.floor(turns * (1.0 / 96.0) + 0.5)
    v = jnp.where(u > 24.0, 48.0 - u, jnp.where(u < -24.0, -48.0 - u, u))
    x = v * (2.0 * math.pi / 96.0)
    y = x * x
    r = jnp.float32(1.0 / 6227020800.0)
    for c in (-1.0 / 39916800.0, 1.0 / 362880.0, -1.0 / 5040.0, 1.0 / 120.0, -1.0 / 6.0, 1.0):
        r = r * y + c
    return x * r


def cosine(turns):
    return sine(turns + 24.0)


def cmul(a, b):
    return (a[0] * b[0] - a[1] * b[1], a[0] * b[1] + a[1] * b[0])


def cadd(a, b):
    return (a[0] + b[0], a[1] + b[1])


def csub(a, b):
    return (a[0] - b[0], a[1] - b[1])


def start_loads(s_hbm, buf, sem):
    for t in range(3):
        for c in range(4 * t, 4 * t + 4):
            pltpu.make_async_copy(
                s_hbm.at[:, :, :, :, pl.ds(128 * c, 128)], buf.at[:, :, :, c], sem.at[t]
            ).start()


def wait_load(buf, sem, t):
    part = buf.at[:, :, :, 4 * t : 4 * t + 4]
    pltpu.make_async_copy(part, part, sem.at[t]).wait()


def fill_phases(mom, rhs, tab):
    x3 = lax.broadcasted_iota(jnp.int32, (96, 128), 0).astype(jnp.float32)
    c3 = cosine(mom[2:3] * x3)
    s3 = sine(mom[2:3] * x3)
    x2 = lax.broadcasted_iota(jnp.int32, (16, 128), 0).astype(jnp.float32)
    tab[0] = cosine(mom[1:2] * x2)
    tab[1] = sine(mom[1:2] * x2)

    def row(b, _):
        c2 = tab[0, pl.ds(b, 1), :]
        s2 = tab[1, pl.ds(b, 1), :]
        at = pl.ds(pl.multiple_of(96 * b, 96), 96)
        rhs[at, 0:128] = (c2 * c3 - s2 * s3).astype(jnp.bfloat16)
        rhs[at, 128:256] = (s2 * c3 + c2 * s3).astype(jnp.bfloat16)
        return 0

    lax.fori_loop(0, 16, row, 0)


def blocks(t, y, buf, sem, wide, skp, lhs):
    low = lax.broadcasted_iota(jnp.int32, (8, 128), 0) < 4

    def rot(v):
        return pltpu.roll(v, 4, 0)

    def widen(i, _):
        for part in range(2):
            for row in range(12):
                wide[part, row, i] = (
                    buf[part, row, i, 4 * t : 4 * t + 4].reshape(16, 128).astype(jnp.float32)
                )
        return 0

    def load(part, row, i, h):
        return wide[part, row, i, 8 * h : 8 * h + 8]

    def pack_k(kp, _):
        for c in range(3):
            made = []
            for part in range(2):
                four = []
                for h in range(2):
                    ah = load(part, 4 * c, 2 * kp, h)
                    bh = load(part, 4 * c, 2 * kp + 1, h)
                    four.append(jnp.where(low, ah, rot(bh)))
                    four.append(jnp.where(low, rot(ah), bh))
                made.append(four)
            for ch in range(4):
                re, im = made[0][ch], made[1][ch]
                skp[ch, 0, c, kp] = re
                skp[ch, 1, c, kp] = im
                skp[ch, 2, c, kp] = re + im
        return 0

    def spins(idx, h):
        return [
            [(load(0, 4 * a + s, idx, h), load(1, 4 * a + s, idx, h)) for s in range(4)]
            for a in range(3)
        ]

    def pair(p, _):
        e = PAIRS * y + p
        d = e // 12
        i = e - 12 * d
        j = lax.rem(i + d, 12)
        for h in range(2):
            xh, yh = spins(i, h), spins(j, h)
            q = {}
            for a, b, c in COLOURS:
                total = None
                for s, u in ((0, 1), (2, 3)):
                    term = csub(cmul(xh[a][s], yh[b][u]), cmul(xh[a][u], yh[b][s]))
                    more = csub(cmul(yh[a][s], xh[b][u]), cmul(yh[a][u], xh[b][s]))
                    term = cadd(term, more)
                    total = term if total is None else cadd(total, term)
                re, im = total
                q[c] = (re, im)
            for odd in range(2):
                ch = 2 * h + odd
                dup = {}
                for c in range(3):
                    both = []
                    for v in q[c]:
                        r = rot(v)
                        both.append(jnp.where(low, r, v) if odd else jnp.where(low, v, r))
                    dup[c] = both + [both[0] + both[1]]
                for kq in range(3):
                    halves = []
                    for kp in (2 * kq, 2 * kq + 1):
                        tot = []
                        for part in range(3):
                            tot.append(
                                dup[0][part] * skp[ch, part, 0, kp]
                                + dup[1][part] * skp[ch, part, 1, kp]
                                + dup[2][part] * skp[ch, part, 2, kp]
                            )
                        halves.append((tot[0] - tot[1], tot[2] - tot[0] - tot[1]))
                    for part in range(2):
                        rows = pl.ds(pl.multiple_of(96 * p + 48 * part + 16 * kq, 16), 16)
                        lanes = slice(512 * t + 128 * ch, 512 * t + 128 * ch + 128)
                        lhs[rows, lanes] = jnp.concatenate(
                            [halves[0][part], halves[1][part]], axis=0
                        ).astype(jnp.bfloat16)
        return 0

    wait_load(buf, sem, t)
    lax.fori_loop(0, 12, widen, 0)
    lax.fori_loop(0, 6, pack_k, 0)
    lax.fori_loop(0, PAIRS, pair, 0)


def finish(mom, x0, y0, scale, chan, acc, zbuf, part1):
    x1 = lax.broadcasted_iota(jnp.int32, (8, 128), 0) % 4 + x0
    turns = mom[0:1] * x1.astype(jnp.float32) + mom[1:2] * y0.astype(jnp.float32)
    fc, fs = cosine(turns) * scale, sine(turns) * scale

    def pair(p, _):
        for g in range(6):
            r = acc[pl.ds(pl.multiple_of(96 * p + 8 * g, 8), 8), :]
            m = acc[pl.ds(pl.multiple_of(96 * p + 48 + 8 * g, 8), 8), :]
            re = r[:, :128] + m[:, 128:]
            im = m[:, :128] - r[:, 128:]
            at = pl.ds(pl.multiple_of(48 * p + 8 * g, 8), 8)
            zbuf[0, at, :] = fc * re + fs * im
            zbuf[1, at, :] = fc * im - fs * re
        return 0

    lax.fori_loop(0, PAIRS, pair, 0)
    zbuf[:, 480:512, :] = jnp.zeros((2, 32, 128), jnp.float32)
    for part in range(2):
        tot = zbuf[part, pl.ds(0, 128, stride=4), :]
        for k in range(1, 4):
            tot = tot + zbuf[part, pl.ds(k, 128, stride=4), :]
        turned = tot.T
        for g in range(8):
            part1[g, IM * part : IM * part + 16, :] = turned[16 * g : 16 * g + 16]
    for g in range(8):
        for k in range(4):
            n = chan[k % 2, 2 * g + k // 2]
            for part in range(2):
                row = part1[pl.ds(n // 16, 1), pl.ds(IM * part + n % 16, 1), :]
                at = 16 + 2 * k + part
                part1[g : g + 1, at : at + 1, :] = row


def place(m):
    i = jnp.floor((m + 0.5) * (1.0 / 144.0))
    r = m - 144.0 * i
    j = jnp.floor((r + 0.5) * (1.0 / 12.0))
    k = r - 12.0 * j
    d = j - i
    d = jnp.where(d < 0.0, d + 12.0, d)
    flip = (d > 6.0) | ((d == 6.0) & (i >= 6.0))
    e = jnp.where(flip, 12.0 * (12.0 - d) + j, 12.0 * d + i)
    slot = jnp.floor((e + 0.5) * (1.0 / PAIRS))
    return slot, (e - PAIRS * slot) * 12.0 + k


def pick(x, lane):
    return jnp.take_along_axis(x, lane, axis=1, mode="promise_in_bounds")


def kernel(
    s_hbm, momenta_hbm, chan_hbm, tindex_hbm, tweight_hbm, lengths_hbm, out, corr,
    buf, wide, rhs, tab, skp, lhs, acc, zbuf, momenta, chan, tindex, tweight, lengths,
    mom_box, term_box, term_all, part1, got1, sum1, got2, part3, got3, cols,
    load_sem, small_sem, send_sem, recv_sem,
):
    sx, x, y = lax.axis_index("sx"), lax.axis_index("sy"), lax.axis_index("mom")
    z, core = sx // 2, lax.rem(sx, 2)
    b = 4 * core + x

    def b_dev(g, plane):
        return (2 * z + g // 4, lax.rem(g, 4), plane)

    def z_dev(g):
        return (2 * g + core, x, y)

    def y_dev(g):
        return (sx, x, g)

    def step(v, o):
        return lax.rem(v + o, 8)

    def copy(src, dst, stage, o, dev, arrive=None):
        return pltpu.make_async_remote_copy(
            src_ref=src, dst_ref=dst, send_sem=send_sem.at[stage, o],
            recv_sem=recv_sem.at[stage, o if arrive is None else arrive], device_id=dev,
            device_id_type=pl.DeviceIdType.MESH,
        )

    smalls = [
        pltpu.make_async_copy(src, dst, small_sem.at[k])
        for k, (src, dst) in enumerate(
            (
                (momenta_hbm, momenta), (tindex_hbm, tindex), (tweight_hbm, tweight),
                (lengths_hbm, lengths), (chan_hbm, chan),
            )
        )
    ]
    for c in smalls:
        c.start()
    start_loads(s_hbm, buf, load_sem)
    barrier = pltpu.get_barrier_semaphore()

    def greet(dev):
        pl.semaphore_signal(barrier, inc=1, device_id=dev, device_id_type=pl.DeviceIdType.MESH)

    alone = b == y
    for o in range(1, 8):
        greet(b_dev(step(b, o), y))
        greet(z_dev(step(z, o)))
        greet(y_dev(step(y, o)))
        greet(b_dev(y, step(y, o)))

    @pl.when(jnp.logical_not(alone))
    def _():
        greet(b_dev(y, y))

    rows = lax.broadcasted_iota(jnp.int32, (8, 128), 0)
    lanes = lax.broadcasted_iota(jnp.int32, (8, 128), 1)
    for c in smalls:
        c.wait()
    mom_box[0] = jnp.zeros((8, 128), jnp.float32)
    mom_box[0, 0:3, 0:16] = momenta[...].astype(jnp.float32)
    mom_box[0] = pltpu.roll(mom_box[0], 16 * y, 1)
    term_box[0] = jnp.zeros((8, 128), jnp.float32)
    live = lax.broadcasted_iota(jnp.int32, (2, 24), 1) + (8 * z + b) * 24
    owner = lax.broadcasted_iota(jnp.int32, (2, 24), 0)
    size = jnp.where(owner == 0, lengths[0], lengths[1])
    for side in range(2):
        slot, lane = place(tindex[side].astype(jnp.float32))
        term_box[0, 2 * side : 2 * side + 2, 0:24] = slot * 128.0 + lane
    term_box[0, 4:6, 0:24] = jnp.where(live < size, tweight[...], 0.0)
    term_box[0] = pltpu.roll(term_box[0], 32 * lax.rem(b, 4), 1)
    slot, lane = place((lanes + 54 * (8 * lax.rem(z, 4) + rows)).astype(jnp.float32))
    cols[0] = slot
    cols[1] = lane

    blocks(0, y, buf, load_sem, wide, skp, lhs)

    pl.semaphore_wait(barrier, jnp.where(alone, 28, 29))
    sent = []
    for o in range(1, 8):
        c = copy(mom_box.at[0], mom_box.at[o], 0, o, y_dev(step(y, o)))
        c.start()
        sent.append(c)
    boxes = []
    for o in range(1, 8):
        c = copy(term_box.at[0], term_box.at[o], 1, o, b_dev(step(b, o), y))
        c.start()
        boxes.append(c)

    blocks(1, y, buf, load_sem, wide, skp, lhs)

    for c in boxes:
        c.wait_recv()
    for half in range(2):
        joined = jnp.zeros((8, 128), jnp.float32)
        for o in range(8):
            source = lax.rem(b + 8 - o, 8)
            joined = joined + jnp.where(source // 4 == half, term_box[o], 0.0)
        term_all[z, half] = joined
    sent += boxes
    boxes = []
    for o in range(1, 8):
        c = copy(term_all.at[z], term_all.at[z], 2, o, z_dev(step(z, o)))
        c.start()
        boxes.append(c)

    blocks(2, y, buf, load_sem, wide, skp, lhs)
    for c in sent[:7]:
        c.wait_recv()
    mom = mom_box[0]
    for o in range(1, 8):
        mom = mom + mom_box[o]
    fill_phases(mom, rhs, tab)
    acc[...] = jnp.dot(lhs[...], rhs[...], preferred_element_type=jnp.float32)
    finish(mom, 4 * sx, 16 * x, SCALE, chan, acc, zbuf, part1)

    hops = []
    for o in range(1, 8):
        g = step(b, o)
        c = copy(part1.at[g], got1.at[o], 3, o, b_dev(g, y))
        c.start()
        hops.append(c)
    total = part1[b]
    for c in hops:
        c.wait_recv()
    for o in range(1, 8):
        total = total + got1[o]
    sum1[...] = total
    sent += hops

    hops = []
    for o in range(1, 8):
        g = step(z, o)
        c = copy(
            sum1.at[pl.ds(pl.multiple_of(16 * (g // 4), 8), 24)], got2.at[o], 4, o, z_dev(g)
        )
        c.start()
        hops.append(c)
    low = z < 4
    total = jnp.where(low, sum1[0:24], sum1[16:40])
    for c in boxes:
        c.wait_recv()
    sent += boxes
    for c in hops:
        c.wait_recv()
    for o in range(1, 8):
        total = total + got2[o]
    sent += hops
    table = jnp.where(low, total[0:16], total[8:24])
    rest = jnp.where(low, total[16:24], total[0:8])
    for g in range(8):
        lane = jnp.broadcast_to(cols[1, g : g + 1], (8, 128)).astype(jnp.int32)
        mine = jnp.broadcast_to(cols[0, g : g + 1], (8, 128)) == y.astype(jnp.float32)
        for u in range(2):
            part3[g, 8 * u : 8 * u + 8] = jnp.where(mine, pick(table[8 * u : 8 * u + 8], lane), 0.0)
        part3[g, 16:24] = rest

    def third(o, arrive):
        g = step(b, o)
        return copy(part3.at[g], got3.at[arrive], 5, o, b_dev(g, b), arrive)

    for o in range(1, 8):
        third(o, y).start()

    @pl.when(jnp.logical_not(alone))
    def _():
        third(0, y).start()

    @pl.when(alone)
    def _():
        got3[y] = part3[y]

    terms = [term_all[:, :, k, :].reshape(16, 128) for k in range(6)]
    places = []
    for k in range(4):
        slot = jnp.floor((terms[k] + 0.5) * (1.0 / 128.0))
        places.append((slot, (terms[k] - 128.0 * slot).astype(jnp.int32)))

    for k in range(8):
        @pl.when(jnp.logical_not(alone & (y == k)))
        def _():
            third(0, k).wait_recv()

    whole = got3[0, 0:16]
    for k in range(1, 8):
        whole = whole + got3[k, 0:16]
    out[...] = whole[:, :54]

    answer = jnp.zeros((2, 2), jnp.float32)
    at_row = lax.broadcasted_iota(jnp.int32, (2, 2), 0)
    at_col = lax.broadcasted_iota(jnp.int32, (2, 2), 1)
    for h in range(2):
        sides = []
        for side in range(2):
            slot, lane = places[2 * side + h]
            both = []
            for part in range(2):
                row = 16 + 4 * h + 2 * side + part
                chosen = []
                for u in range(2):
                    value = jnp.zeros((8, 128), jnp.float32)
                    for k in range(8):
                        have = jnp.broadcast_to(got3[k, row : row + 1], (8, 128))
                        have = pick(have, lane[8 * u : 8 * u + 8])
                        value = jnp.where(slot[8 * u : 8 * u + 8] == k, have, value)
                    chosen.append(value)
                both.append(jnp.concatenate(chosen, axis=0))
            sides.append(tuple(both))
        prod = cmul(sides[0], sides[1])
        for part in range(2):
            answer = jnp.where(
                (at_row == part) & (at_col == h), jnp.sum(terms[4 + h] * prod[part]), answer
            )
    corr[...] = answer

    for c in sent:
        c.wait_send()
    for o in range(1, 8):
        third(o, y).wait_send()

    @pl.when(jnp.logical_not(alone))
    def _():
        third(0, y).wait_send()


def local(propagator, momenta, chan_moms, term_index, term_weight, lengths):
    f32, i32 = jnp.float32, jnp.int32
    vmem = pl.BlockSpec(memory_space=pltpu.VMEM)
    return pl.pallas_call(
        kernel,
        out_shape=(
            jax.ShapeDtypeStruct((16, 54), f32),
            jax.ShapeDtypeStruct((2, 2), f32),
        ),
        in_specs=[pl.BlockSpec(memory_space=pl.ANY)] * 6,
        out_specs=(vmem, vmem),
        scratch_shapes=[
            pltpu.VMEM((2, 12, 12, 12, 4, 128), jnp.bfloat16),
            pltpu.VMEM((2, 12, 12, 16, 128), f32),
            pltpu.VMEM((1536, 256), jnp.bfloat16),
            pltpu.VMEM((2, 16, 128), f32),
            pltpu.VMEM((4, 3, 3, 6, 8, 128), f32),
            pltpu.VMEM((96 * PAIRS, 1536), jnp.bfloat16),
            pltpu.VMEM((96 * PAIRS, 256), f32),
            pltpu.VMEM((2, 512, 128), f32),
            pltpu.VMEM((3, 16), i32),
            pltpu.SMEM((2, 16), i32),
            pltpu.VMEM((2, 2, 24), i32),
            pltpu.VMEM((2, 24), f32),
            pltpu.SMEM((2,), i32),
            pltpu.VMEM((8, 8, 128), f32),
            pltpu.VMEM((8, 8, 128), f32),
            pltpu.VMEM((8, 2, 8, 128), f32),
            pltpu.VMEM((8, 40, 128), f32),
            pltpu.VMEM((8, 40, 128), f32),
            pltpu.VMEM((40, 128), f32),
            pltpu.VMEM((8, 24, 128), f32),
            pltpu.VMEM((8, 24, 128), f32),
            pltpu.VMEM((8, 24, 128), f32),
            pltpu.VMEM((2, 8, 128), f32),
            pltpu.SemaphoreType.DMA((3,)),
            pltpu.SemaphoreType.DMA((5,)),
            pltpu.SemaphoreType.DMA((6, 8)),
            pltpu.SemaphoreType.DMA((6, 8)),
        ],
        compiler_params=pltpu.CompilerParams(
            collective_id=0, has_side_effects=True, vmem_limit_bytes=62 * 2**20
        ),
    )(propagator, momenta.T, chan_moms.T, term_index, term_weight, lengths)


def solution(mesh):
    in_specs = (
        P(None, None, None, "sx", "sy"),
        P("mom", None),
        P(),
        P(None, "mom", ("sx", "sy")),
        P("mom", ("sx", "sy")),
        P("mom"),
    )
    out_specs = (P("mom", ("sx", "sy")), P(None, "mom"))
    return jax.shard_map(local, mesh=mesh, in_specs=in_specs, out_specs=out_specs, check_vma=False)
```

```python
import math
import jax
import jax.numpy as jnp
from jax import lax
from jax.experimental import pallas as pl
from jax.experimental.pallas import tpu as pltpu
from jax.sharding import PartitionSpec as P

LAT = 96
PAIRS = 10
SCALE = 1.0 / math.sqrt(393216)
IM = 24
COLOURS = ((1, 2, 0), (2, 0, 1), (0, 1, 2))


def sine(turns):
    u = turns - 96.0 * jnp.floor(turns * (1.0 / 96.0) + 0.5)
    v = jnp.where(u > 24.0, 48.0 - u, jnp.where(u < -24.0, -48.0 - u, u))
    x = v * (2.0 * math.pi / 96.0)
    y = x * x
    r = jnp.float32(1.0 / 6227020800.0)
    for c in (-1.0 / 39916800.0, 1.0 / 362880.0, -1.0 / 5040.0, 1.0 / 120.0, -1.0 / 6.0, 1.0):
        r = r * y + c
    return x * r


def cosine(turns):
    return sine(turns + 24.0)


def cmul(a, b):
    return (a[0] * b[0] - a[1] * b[1], a[0] * b[1] + a[1] * b[0])


def cadd(a, b):
    return (a[0] + b[0], a[1] + b[1])


def csub(a, b):
    return (a[0] - b[0], a[1] - b[1])


def start_loads(s_hbm, buf, sem):
    for t in range(3):
        for c in range(4 * t, 4 * t + 4):
            pltpu.make_async_copy(
                s_hbm.at[:, :, :, :, pl.ds(128 * c, 128)], buf.at[:, :, :, c], sem.at[t]
            ).start()


def wait_load(buf, sem, t):
    part = buf.at[:, :, :, 4 * t : 4 * t + 4]
    pltpu.make_async_copy(part, part, sem.at[t]).wait()


def fill_phases(rhs, tab):
    lane = lax.broadcasted_iota(jnp.int32, (1, 128), 1).astype(jnp.float32)
    p2 = jnp.floor((lane + 0.5) * (1.0 / 9.0))
    p3 = lane - 9.0 * p2 - 4.0
    p2 = p2 - 4.0
    x3 = lax.broadcasted_iota(jnp.int32, (96, 128), 0).astype(jnp.float32)
    c3 = cosine(p3 * x3)
    s3 = sine(p3 * x3)
    x2 = lax.broadcasted_iota(jnp.int32, (16, 128), 0).astype(jnp.float32)
    tab[0] = cosine(p2 * x2)
    tab[1] = sine(p2 * x2)

    def row(b, _):
        c2 = tab[0, pl.ds(b, 1), :]
        s2 = tab[1, pl.ds(b, 1), :]
        at = pl.ds(pl.multiple_of(96 * b, 96), 96)
        rhs[at, 0:128] = (c2 * c3 - s2 * s3).astype(jnp.bfloat16)
        rhs[at, 128:256] = (s2 * c3 + c2 * s3).astype(jnp.bfloat16)
        return 0

    lax.fori_loop(0, 16, row, 0)


def blocks(t, y, buf, sem, wide, skp, lhs):
    low = lax.broadcasted_iota(jnp.int32, (8, 128), 0) < 4

    def rot(v):
        return pltpu.roll(v, 4, 0)

    def widen(i, _):
        for part in range(2):
            for row in range(12):
                wide[part, row, i] = (
                    buf[part, row, i, 4 * t : 4 * t + 4].reshape(16, 128).astype(jnp.float32)
                )
        return 0

    def load(part, row, i, h):
        return wide[part, row, i, 8 * h : 8 * h + 8]

    def pack_k(kp, _):
        for c in range(3):
            made = []
            for part in range(2):
                four = []
                for h in range(2):
                    ah = load(part, 4 * c, 2 * kp, h)
                    bh = load(part, 4 * c, 2 * kp + 1, h)
                    four.append(jnp.where(low, ah, rot(bh)))
                    four.append(jnp.where(low, rot(ah), bh))
                made.append(four)
            for ch in range(4):
                re, im = made[0][ch], made[1][ch]
                skp[ch, 0, c, kp] = re
                skp[ch, 1, c, kp] = im
                skp[ch, 2, c, kp] = re + im
        return 0

    def spins(idx, h):
        return [
            [(load(0, 4 * a + s, idx, h), load(1, 4 * a + s, idx, h)) for s in range(4)]
            for a in range(3)
        ]

    def pair(p, _):
        e = PAIRS * y + p
        d = e // 12
        i = e - 12 * d
        j = lax.rem(i + d, 12)
        for h in range(2):
            xh, yh = spins(i, h), spins(j, h)
            q = {}
            for a, b, c in COLOURS:
                total = None
                for s, u in ((0, 1), (2, 3)):
                    term = csub(cmul(xh[a][s], yh[b][u]), cmul(xh[a][u], yh[b][s]))
                    more = csub(cmul(yh[a][s], xh[b][u]), cmul(yh[a][u], xh[b][s]))
                    term = cadd(term, more)
                    total = term if total is None else cadd(total, term)
                re, im = total
                q[c] = (re, im)
            for odd in range(2):
                ch = 2 * h + odd
                dup = {}
                for c in range(3):
                    both = []
                    for v in q[c]:
                        r = rot(v)
                        both.append(jnp.where(low, r, v) if odd else jnp.where(low, v, r))
                    dup[c] = both + [both[0] + both[1]]
                for kq in range(3):
                    halves = []
                    for kp in (2 * kq, 2 * kq + 1):
                        tot = []
                        for part in range(3):
                            tot.append(
                                dup[0][part] * skp[ch, part, 0, kp]
                                + dup[1][part] * skp[ch, part, 1, kp]
                                + dup[2][part] * skp[ch, part, 2, kp]
                            )
                        halves.append((tot[0] - tot[1], tot[2] - tot[0] - tot[1]))
                    for part in range(2):
                        rows = pl.ds(pl.multiple_of(96 * p + 48 * part + 16 * kq, 16), 16)
                        lanes = slice(512 * t + 128 * ch, 512 * t + 128 * ch + 128)
                        lhs[rows, lanes] = jnp.concatenate(
                            [halves[0][part], halves[1][part]], axis=0
                        ).astype(jnp.bfloat16)
        return 0

    wait_load(buf, sem, t)
    lax.fori_loop(0, 12, widen, 0)
    lax.fori_loop(0, 6, pack_k, 0)
    lax.fori_loop(0, PAIRS, pair, 0, unroll=2)


def pick(x, lane):
    return jnp.take_along_axis(x, lane, axis=1, mode="promise_in_bounds")


def finish(mom, x0, y0, scale, chan, acc, zbuf, part1):
    x1 = lax.broadcasted_iota(jnp.int32, (8, 128), 0) % 4 + x0
    turns = mom[0:1] * x1.astype(jnp.float32) + mom[1:2] * y0.astype(jnp.float32)
    fc, fs = cosine(turns) * scale, sine(turns) * scale
    cell = (9.0 * mom[1:2] + mom[2:3] + 40.0).astype(jnp.int32)
    cell = jnp.broadcast_to(cell, (8, 128))

    def pair(p, _):
        for g in range(6):
            r = acc[pl.ds(pl.multiple_of(96 * p + 8 * g, 8), 8), :]
            m = acc[pl.ds(pl.multiple_of(96 * p + 48 + 8 * g, 8), 8), :]
            re = pick(r[:, :128] + m[:, 128:], cell)
            im = pick(m[:, :128] - r[:, 128:], cell)
            at = pl.ds(pl.multiple_of(48 * p + 8 * g, 8), 8)
            zbuf[0, at, :] = fc * re + fs * im
            zbuf[1, at, :] = fc * im - fs * re
        return 0

    lax.fori_loop(0, PAIRS, pair, 0)
    zbuf[:, 480:512, :] = jnp.zeros((2, 32, 128), jnp.float32)
    for part in range(2):
        tot = zbuf[part, pl.ds(0, 128, stride=4), :]
        for k in range(1, 4):
            tot = tot + zbuf[part, pl.ds(k, 128, stride=4), :]
        turned = tot.T
        for g in range(8):
            part1[g, IM * part : IM * part + 16, :] = turned[16 * g : 16 * g + 16]
    for g in range(8):
        for k in range(4):
            n = chan[k % 2, 2 * g + k // 2]
            for part in range(2):
                row = part1[pl.ds(n // 16, 1), pl.ds(IM * part + n % 16, 1), :]
                at = 16 + 2 * k + part
                part1[g : g + 1, at : at + 1, :] = row


def locate(m):
    i = jnp.floor((m + 0.5) * (1.0 / 144.0))
    r = m - 144.0 * i
    j = jnp.floor((r + 0.5) * (1.0 / 12.0))
    k = r - 12.0 * j
    d = j - i
    d = jnp.where(d < 0.0, d + 12.0, d)
    flip = (d > 6.0) | ((d == 6.0) & (i >= 6.0))
    e = jnp.where(flip, 12.0 * (12.0 - d) + j, 12.0 * d + i)
    slot = jnp.floor((e + 0.5) * (1.0 / PAIRS))
    odd = i - 2.0 * jnp.floor(0.5 * i)
    kind = jnp.where(flip, 1.0 - odd, odd)
    return slot, e - PAIRS * slot, k, kind


def place(m):
    slot, inner, k, _ = locate(m)
    return slot, inner * 12.0 + k


def kernel(
    s_hbm, momenta_hbm, chan_hbm, tindex_hbm, tweight_hbm, lengths_hbm, out, corr,
    buf, wide, rhs, tab, skp, lhs, acc, zbuf, momenta, chan, tindex, tweight, lengths,
    mom_box, term_box, term_all, part1, got1, sum1, got2, part3, got3, cols,
    load_sem, small_sem, send_sem, recv_sem,
):
    sx, x, y = lax.axis_index("sx"), lax.axis_index("sy"), lax.axis_index("mom")
    z, core = sx // 2, lax.rem(sx, 2)
    b = 4 * core + x

    def b_dev(g, plane):
        return (2 * z + g // 4, lax.rem(g, 4), plane)

    def z_dev(g):
        return (2 * g + core, x, y)

    def y_dev(g):
        return (sx, x, g)

    def step(v, o):
        return lax.rem(v + o, 8)

    def copy(src, dst, stage, o, dev, arrive=None):
        return pltpu.make_async_remote_copy(
            src_ref=src, dst_ref=dst, send_sem=send_sem.at[stage, o],
            recv_sem=recv_sem.at[stage, o if arrive is None else arrive], device_id=dev,
            device_id_type=pl.DeviceIdType.MESH,
        )

    smalls = [
        pltpu.make_async_copy(src, dst, small_sem.at[k])
        for k, (src, dst) in enumerate(
            (
                (momenta_hbm, momenta), (tindex_hbm, tindex), (tweight_hbm, tweight),
                (lengths_hbm, lengths), (chan_hbm, chan),
            )
        )
    ]
    for c in smalls:
        c.start()
    start_loads(s_hbm, buf, load_sem)
    barrier = pltpu.get_barrier_semaphore()

    def greet(dev):
        pl.semaphore_signal(barrier, inc=1, device_id=dev, device_id_type=pl.DeviceIdType.MESH)

    alone = b == y
    for o in range(1, 8):
        greet(b_dev(step(b, o), y))
        greet(z_dev(step(z, o)))
        greet(y_dev(step(y, o)))
        greet(b_dev(y, step(y, o)))

    @pl.when(jnp.logical_not(alone))
    def _():
        greet(b_dev(y, y))

    fill_phases(rhs, tab)
    rows = lax.broadcasted_iota(jnp.int32, (8, 128), 0)
    lanes = lax.broadcasted_iota(jnp.int32, (8, 128), 1)
    for c in smalls:
        c.wait()
    mom_box[0] = jnp.zeros((8, 128), jnp.float32)
    mom_box[0, 0:3, 0:16] = momenta[...].astype(jnp.float32)
    mom_box[0] = pltpu.roll(mom_box[0], 16 * y, 1)
    term_box[0] = jnp.zeros((8, 128), jnp.float32)
    live = lax.broadcasted_iota(jnp.int32, (2, 24), 1) + (8 * z + b) * 24
    owner = lax.broadcasted_iota(jnp.int32, (2, 24), 0)
    size = jnp.where(owner == 0, lengths[0], lengths[1])
    for side in range(2):
        slot, lane = place(tindex[side].astype(jnp.float32))
        term_box[0, 2 * side : 2 * side + 2, 0:24] = slot * 128.0 + lane
    term_box[0, 4:6, 0:24] = jnp.where(live < size, tweight[...], 0.0)
    term_box[0] = pltpu.roll(term_box[0], 32 * lax.rem(b, 4), 1)
    slot, inner, k, kind = locate((lanes + 54 * (8 * lax.rem(z, 4) + rows)).astype(jnp.float32))
    mine = (slot == y.astype(jnp.float32)) & (lanes < 54)
    held = [
        jnp.max(jnp.where(mine & (kind == v), inner, 0.0), axis=1, keepdims=True) for v in range(2)
    ]
    within = lax.rem(lanes, 32)
    second = within >= 12
    cols[0] = jnp.where(second, held[1], held[0]) * 12.0 + jnp.where(
        second, within - 12, within
    ).astype(jnp.float32)
    cols[1] = slot
    cols[2] = 12.0 * kind + k

    blocks(0, y, buf, load_sem, wide, skp, lhs)

    pl.semaphore_wait(barrier, jnp.where(alone, 28, 29))
    sent = []
    for o in range(1, 8):
        c = copy(mom_box.at[0], mom_box.at[o], 0, o, y_dev(step(y, o)))
        c.start()
        sent.append(c)
    boxes = []
    for o in range(1, 8):
        c = copy(term_box.at[0], term_box.at[o], 1, o, b_dev(step(b, o), y))
        c.start()
        boxes.append(c)

    blocks(1, y, buf, load_sem, wide, skp, lhs)

    blocks(2, y, buf, load_sem, wide, skp, lhs)
    acc[...] = jnp.dot(lhs[...], rhs[...], preferred_element_type=jnp.float32)
    for c in sent[:7]:
        c.wait_recv()
    mom = mom_box[0]
    for o in range(1, 8):
        mom = mom + mom_box[o]
    finish(mom, 4 * sx, 16 * x, SCALE, chan, acc, zbuf, part1)

    hops = []
    for o in range(1, 8):
        g = step(b, o)
        c = copy(part1.at[g], got1.at[o], 3, o, b_dev(g, y))
        c.start()
        hops.append(c)
    for c in boxes:
        c.wait_recv()
    for half in range(2):
        joined = jnp.zeros((8, 128), jnp.float32)
        for o in range(8):
            source = lax.rem(b + 8 - o, 8)
            joined = joined + jnp.where(source // 4 == half, term_box[o], 0.0)
        term_all[z, half] = joined
    sent += boxes
    boxes = []
    for o in range(1, 8):
        c = copy(term_all.at[z], term_all.at[z], 2, o, z_dev(step(z, o)))
        c.start()
        boxes.append(c)
    total = part1[b]
    for c in hops:
        c.wait_recv()
    for o in range(1, 8):
        total = total + got1[o]
    sum1[...] = total
    sent += hops

    hops = []
    for o in range(1, 8):
        g = step(z, o)
        c = copy(
            sum1.at[pl.ds(pl.multiple_of(16 * (g // 4), 8), 24)], got2.at[o], 4, o, z_dev(g)
        )
        c.start()
        hops.append(c)
    low = z < 4
    total = jnp.where(low, sum1[0:24], sum1[16:40])
    for c in hops:
        c.wait_recv()
    for o in range(1, 8):
        total = total + got2[o]
    sent += hops
    table = jnp.where(low, total[0:16], total[8:24])
    rest = jnp.where(low, total[16:24], total[0:8])
    for g in range(8):
        lane = jnp.broadcast_to(cols[0, g : g + 1], (8, 128)).astype(jnp.int32)
        packed = []
        for u in range(2):
            have = pick(table[8 * u : 8 * u + 8], lane)
            packed.append(jnp.where(lax.rem(lanes // 32, 2) == 1, pltpu.roll(have, 4, 0), have))
        part3[g, 0:8] = rest
        part3[g, 8:12] = jnp.where(lanes < 64, packed[0], packed[1])[0:4]

    def third(o, arrive):
        g = step(b, o)
        return copy(part3.at[g], got3.at[arrive], 5, o, b_dev(g, b), arrive)

    for o in range(1, 8):
        third(o, y).start()

    @pl.when(jnp.logical_not(alone))
    def _():
        third(0, y).start()

    @pl.when(alone)
    def _():
        got3[y] = part3[y]

    for c in boxes:
        c.wait_recv()
    sent += boxes
    terms = [term_all[:, :, k, :].reshape(16, 128) for k in range(6)]
    places = []
    for k in range(4):
        slot = jnp.floor((terms[k] + 0.5) * (1.0 / 128.0))
        places.append((slot, (terms[k] - 128.0 * slot).astype(jnp.int32)))

    for k in range(8):
        @pl.when(jnp.logical_not(alone & (y == k)))
        def _():
            third(0, k).wait_recv()

    slot = jnp.broadcast_to(cols[1, pl.ds(b, 1), :], (8, 128))
    lane = jnp.broadcast_to(cols[2, pl.ds(b, 1), :], (8, 128)).astype(jnp.int32)
    quads = [jnp.zeros((8, 128), jnp.float32) for g in range(4)]
    for v in range(4):
        have = jnp.concatenate([got3[2 * v, 8:12], got3[2 * v + 1, 8:12]], axis=0)
        here = slot == jnp.where(rows < 4, 2.0 * v, 2.0 * v + 1.0)
        for g in range(4):
            quads[g] = jnp.where(here, pick(have, lane + 32 * g), quads[g])
    for g in range(4):
        whole = quads[g] + pltpu.roll(quads[g], 4, 0)
        out[4 * g : 4 * g + 4, :] = whole[0:4, :54]

    answer = jnp.zeros((2, 2), jnp.float32)
    at_row = lax.broadcasted_iota(jnp.int32, (2, 2), 0)
    at_col = lax.broadcasted_iota(jnp.int32, (2, 2), 1)
    for h in range(2):
        sides = []
        for side in range(2):
            slot, lane = places[2 * side + h]
            both = []
            for part in range(2):
                row = 4 * h + 2 * side + part
                chosen = []
                for u in range(2):
                    value = jnp.zeros((8, 128), jnp.float32)
                    for k in range(8):
                        have = jnp.broadcast_to(got3[k, row : row + 1], (8, 128))
                        have = pick(have, lane[8 * u : 8 * u + 8])
                        value = jnp.where(slot[8 * u : 8 * u + 8] == k, have, value)
                    chosen.append(value)
                both.append(jnp.concatenate(chosen, axis=0))
            sides.append(tuple(both))
        prod = cmul(sides[0], sides[1])
        for part in range(2):
            answer = jnp.where(
                (at_row == part) & (at_col == h), jnp.sum(terms[4 + h] * prod[part]), answer
            )
    corr[...] = answer

    for c in sent:
        c.wait_send()
    for o in range(1, 8):
        third(o, y).wait_send()

    @pl.when(jnp.logical_not(alone))
    def _():
        third(0, y).wait_send()


def hand_over(block, value, out, corr, sem):
    copies = [
        pltpu.make_async_copy(block, out, sem.at[0]),
        pltpu.make_async_copy(value, corr, sem.at[1]),
    ]
    for c in copies:
        c.start()
    for c in copies:
        c.wait()


def local(propagator, momenta, chan_moms, term_index, term_weight, lengths):
    f32, i32 = jnp.float32, jnp.int32
    vmem = pl.BlockSpec(memory_space=pltpu.VMEM)
    results = pl.pallas_call(
        kernel,
        out_shape=(
            pltpu.VMEM((16, 54), f32),
            pltpu.VMEM((2, 2), f32),
        ),
        in_specs=[pl.BlockSpec(memory_space=pl.ANY)] * 6,
        out_specs=(vmem, vmem),
        scratch_shapes=[
            pltpu.VMEM((2, 12, 12, 12, 4, 128), jnp.bfloat16),
            pltpu.VMEM((2, 12, 12, 16, 128), f32),
            pltpu.VMEM((1536, 256), jnp.bfloat16),
            pltpu.VMEM((2, 16, 128), f32),
            pltpu.VMEM((4, 3, 3, 6, 8, 128), f32),
            pltpu.VMEM((96 * PAIRS, 1536), jnp.bfloat16),
            pltpu.VMEM((96 * PAIRS, 256), f32),
            pltpu.VMEM((2, 512, 128), f32),
            pltpu.VMEM((3, 16), i32),
            pltpu.SMEM((2, 16), i32),
            pltpu.VMEM((2, 2, 24), i32),
            pltpu.VMEM((2, 24), f32),
            pltpu.SMEM((2,), i32),
            pltpu.VMEM((8, 8, 128), f32),
            pltpu.VMEM((8, 8, 128), f32),
            pltpu.VMEM((8, 2, 8, 128), f32),
            pltpu.VMEM((8, 40, 128), f32),
            pltpu.VMEM((8, 40, 128), f32),
            pltpu.VMEM((40, 128), f32),
            pltpu.VMEM((8, 24, 128), f32),
            pltpu.VMEM((8, 12, 128), f32),
            pltpu.VMEM((8, 12, 128), f32),
            pltpu.VMEM((3, 8, 128), f32),
            pltpu.SemaphoreType.DMA((3,)),
            pltpu.SemaphoreType.DMA((5,)),
            pltpu.SemaphoreType.DMA((6, 8)),
            pltpu.SemaphoreType.DMA((6, 8)),
        ],
        compiler_params=pltpu.CompilerParams(
            collective_id=0, has_side_effects=True, vmem_limit_bytes=62 * 2**20
        ),
    )(propagator, momenta.T, chan_moms.T, term_index, term_weight, lengths)
    return pl.pallas_call(
        hand_over,
        out_shape=(
            jax.ShapeDtypeStruct((16, 54), f32),
            jax.ShapeDtypeStruct((2, 2), f32),
        ),
        in_specs=[vmem] * 2,
        out_specs=[pl.BlockSpec(memory_space=pl.ANY)] * 2,
        scratch_shapes=[pltpu.SemaphoreType.DMA((2,))],
        compiler_params=pltpu.CompilerParams(vmem_limit_bytes=2**20),
    )(*results)


def solution(mesh):
    in_specs = (
        P(None, None, None, "sx", "sy"),
        P("mom", None),
        P(),
        P(None, "mom", ("sx", "sy")),
        P("mom", ("sx", "sy")),
        P("mom"),
    )
    out_specs = (P("mom", ("sx", "sy")), P(None, "mom"))
    return jax.shard_map(local, mesh=mesh, in_specs=in_specs, out_specs=out_specs, check_vma=False)
```

```python
import math
import jax
import jax.numpy as jnp
from jax import lax
from jax.experimental import pallas as pl
from jax.experimental.pallas import tpu as pltpu
from jax.sharding import PartitionSpec as P

LAT = 96
PAIRS = 10
SCALE = 1.0 / math.sqrt(393216)
IM = 24
FAR = (4, 3, 5, 2, 6, 1, 7)
COLOURS = ((1, 2, 0), (2, 0, 1), (0, 1, 2))


def sine(turns):
    u = turns - 96.0 * jnp.floor(turns * (1.0 / 96.0) + 0.5)
    v = jnp.where(u > 24.0, 48.0 - u, jnp.where(u < -24.0, -48.0 - u, u))
    x = v * (2.0 * math.pi / 96.0)
    y = x * x
    r = jnp.float32(1.0 / 6227020800.0)
    for c in (-1.0 / 39916800.0, 1.0 / 362880.0, -1.0 / 5040.0, 1.0 / 120.0, -1.0 / 6.0, 1.0):
        r = r * y + c
    return x * r


def cosine(turns):
    return sine(turns + 24.0)


def cmul(a, b):
    return (a[0] * b[0] - a[1] * b[1], a[0] * b[1] + a[1] * b[0])


def cadd(a, b):
    return (a[0] + b[0], a[1] + b[1])


def csub(a, b):
    return (a[0] - b[0], a[1] - b[1])


def start_loads(s_hbm, buf, sem, thirds):
    for t in thirds:
        for c in range(4 * t, 4 * t + 4):
            pltpu.make_async_copy(
                s_hbm.at[:, :, :, :, pl.ds(128 * c, 128)], buf.at[:, :, :, c], sem.at[t]
            ).start()


def wait_load(buf, sem, t):
    part = buf.at[:, :, :, pl.ds(4 * t, 4)]
    pltpu.make_async_copy(part, part, sem.at[t]).wait()


def fill_phases(rhs, tab):
    lane = lax.broadcasted_iota(jnp.int32, (1, 128), 1).astype(jnp.float32)
    p2 = jnp.floor((lane + 0.5) * (1.0 / 9.0))
    p3 = lane - 9.0 * p2 - 4.0
    p2 = p2 - 4.0
    x3 = lax.broadcasted_iota(jnp.int32, (96, 128), 0).astype(jnp.float32)
    c3 = cosine(p3 * x3)
    s3 = sine(p3 * x3)
    x2 = lax.broadcasted_iota(jnp.int32, (16, 128), 0).astype(jnp.float32)
    tab[0] = cosine(p2 * x2)
    tab[1] = sine(p2 * x2)

    def row(b, _):
        c2 = tab[0, pl.ds(b, 1), :]
        s2 = tab[1, pl.ds(b, 1), :]
        at = pl.ds(pl.multiple_of(96 * b, 96), 96)
        rhs[at, 0:128] = (c2 * c3 - s2 * s3).astype(jnp.bfloat16)
        rhs[at, 128:256] = (s2 * c3 + c2 * s3).astype(jnp.bfloat16)
        return 0

    lax.fori_loop(0, 16, row, 0)


def blocks(t, y, buf, sem, wide, skp, lhs, rhs, acc):
    low = lax.broadcasted_iota(jnp.int32, (8, 128), 0) < 4

    def rot(v):
        return pltpu.roll(v, 4, 0)

    def widen(i, _):
        for part in range(2):
            for row in range(12):
                wide[part, row, i] = (
                    buf[part, row, i, pl.ds(4 * t, 4)].reshape(16, 128).astype(jnp.float32)
                )
        return 0

    def load(part, row, i, h):
        return wide[part, row, i, 8 * h : 8 * h + 8]

    def pack_k(kp, _):
        for c in range(3):
            made = []
            for part in range(2):
                four = []
                for h in range(2):
                    ah = load(part, 4 * c, 2 * kp, h)
                    bh = load(part, 4 * c, 2 * kp + 1, h)
                    four.append(jnp.where(low, ah, rot(bh)))
                    four.append(jnp.where(low, rot(ah), bh))
                made.append(four)
            for ch in range(4):
                re, im = made[0][ch], made[1][ch]
                skp[ch, 0, c, kp] = re
                skp[ch, 1, c, kp] = im
                skp[ch, 2, c, kp] = re + im
        return 0

    def spins(idx, h):
        return [
            [(load(0, 4 * a + s, idx, h), load(1, 4 * a + s, idx, h)) for s in range(4)]
            for a in range(3)
        ]

    def pair(p, _):
        e = PAIRS * y + p
        d = e // 12
        i = e - 12 * d
        j = lax.rem(i + d, 12)
        for h in range(2):
            xh, yh = spins(i, h), spins(j, h)
            q = {}
            for a, b, c in COLOURS:
                total = None
                for s, u in ((0, 1), (2, 3)):
                    term = csub(cmul(xh[a][s], yh[b][u]), cmul(xh[a][u], yh[b][s]))
                    more = csub(cmul(yh[a][s], xh[b][u]), cmul(yh[a][u], xh[b][s]))
                    term = cadd(term, more)
                    total = term if total is None else cadd(total, term)
                re, im = total
                q[c] = (re, im)
            for odd in range(2):
                ch = 2 * h + odd
                dup = {}
                for c in range(3):
                    both = []
                    for v in q[c]:
                        r = rot(v)
                        both.append(jnp.where(low, r, v) if odd else jnp.where(low, v, r))
                    dup[c] = both + [both[0] + both[1]]
                for kq in range(3):
                    halves = []
                    for kp in (2 * kq, 2 * kq + 1):
                        tot = []
                        for part in range(3):
                            tot.append(
                                dup[0][part] * skp[ch, part, 0, kp]
                                + dup[1][part] * skp[ch, part, 1, kp]
                                + dup[2][part] * skp[ch, part, 2, kp]
                            )
                        halves.append((tot[0] - tot[1], tot[2] - tot[0] - tot[1]))
                    for part in range(2):
                        rows = pl.ds(pl.multiple_of(96 * p + 48 * part + 16 * kq, 16), 16)
                        lanes = pl.ds(pl.multiple_of(512 * t + 128 * ch, 128), 128)
                        lhs[rows, lanes] = jnp.concatenate(
                            [halves[0][part], halves[1][part]], axis=0
                        ).astype(jnp.bfloat16)
        return 0

    wait_load(buf, sem, t)
    lax.fori_loop(0, 12, widen, 0)
    lax.fori_loop(0, 6, pack_k, 0)
    def two(p, _):
        if t:
            rows = pl.ds(pl.multiple_of(192 * p, 64), 192)
            depth = slice(512 * t - 512, 512 * t)
            prod = jnp.dot(lhs[rows, depth], rhs[depth, :], preferred_element_type=jnp.float32)
            acc[rows, :] = prod if t == 1 else acc[rows, :] + prod
        pair(2 * p, 0)
        pair(2 * p + 1, 0)
        return 0

    lax.fori_loop(0, PAIRS // 2, two, 0)


def pick(x, lane):
    return jnp.take_along_axis(x, lane, axis=1, mode="promise_in_bounds")


def finish(mom, x0, y0, scale, spots, acc, zbuf, part1):
    x1 = lax.broadcasted_iota(jnp.int32, (8, 128), 0) % 4 + x0
    turns = mom[0:1] * x1.astype(jnp.float32) + mom[1:2] * y0.astype(jnp.float32)
    fc, fs = cosine(turns) * scale, sine(turns) * scale
    cell = (9.0 * mom[1:2] + mom[2:3] + 40.0).astype(jnp.int32)
    cell = jnp.broadcast_to(cell, (8, 128))

    def pair(p, _):
        for g in range(6):
            r = acc[pl.ds(pl.multiple_of(96 * p + 8 * g, 8), 8), :]
            m = acc[pl.ds(pl.multiple_of(96 * p + 48 + 8 * g, 8), 8), :]
            re = pick(r[:, :128] + m[:, 128:], cell)
            im = pick(m[:, :128] - r[:, 128:], cell)
            at = pl.ds(pl.multiple_of(48 * p + 8 * g, 8), 8)
            zbuf[0, at, :] = fc * re + fs * im
            zbuf[1, at, :] = fc * im - fs * re
        return 0

    lax.fori_loop(0, PAIRS, pair, 0)
    zbuf[:, 480:512, :] = jnp.zeros((2, 32, 128), jnp.float32)
    for part in range(2):
        tot = zbuf[part, pl.ds(0, 128, stride=4), :]
        for k in range(1, 4):
            tot = tot + zbuf[part, pl.ds(k, 128, stride=4), :]
        turned = tot.T
        for g in range(8):
            part1[40 * g + IM * part : 40 * g + IM * part + 16, :] = turned[16 * g : 16 * g + 16]
    for g in range(8):
        for k in range(4):
            row = spots[4 * g + k]
            for part in range(2):
                at = 40 * g + 16 + 2 * k + part
                part1[at : at + 1, :] = part1[pl.ds(row + IM * part, 1), :]


def locate(m):
    i = jnp.floor((m + 0.5) * (1.0 / 144.0))
    r = m - 144.0 * i
    j = jnp.floor((r + 0.5) * (1.0 / 12.0))
    k = r - 12.0 * j
    d = j - i
    d = jnp.where(d < 0.0, d + 12.0, d)
    flip = (d > 6.0) | ((d == 6.0) & (i >= 6.0))
    e = jnp.where(flip, 12.0 * (12.0 - d) + j, 12.0 * d + i)
    slot = jnp.floor((e + 0.5) * (1.0 / PAIRS))
    odd = i - 2.0 * jnp.floor(0.5 * i)
    kind = jnp.where(flip, 1.0 - odd, odd)
    return slot, e - PAIRS * slot, k, kind


def place(m):
    slot, inner, k, _ = locate(m)
    return slot, inner * 12.0 + k


def kernel(
    s_hbm, momenta_hbm, chan_hbm, tindex_hbm, tweight_hbm, lengths_hbm, out, corr,
    buf, wide, rhs, tab, skp, lhs, acc, zbuf, momenta, chan, spots, tindex, tweight, lengths,
    mom_box, term_box, term_all, part1, got1, sum1, got2, part3, got3, cols,
    load_sem, small_sem, send_sem, recv_sem,
):
    sx, x, y = lax.axis_index("sx"), lax.axis_index("sy"), lax.axis_index("mom")
    z, core = sx // 2, lax.rem(sx, 2)
    b = 4 * core + x

    def b_dev(g, plane):
        return (2 * z + g // 4, lax.rem(g, 4), plane)

    def z_dev(g):
        return (2 * g + core, x, y)

    def y_dev(g):
        return (sx, x, g)

    def step(v, o):
        return lax.rem(v + o, 8)

    def copy(src, dst, stage, o, dev, arrive=None):
        return pltpu.make_async_remote_copy(
            src_ref=src, dst_ref=dst, send_sem=send_sem.at[stage, o],
            recv_sem=recv_sem.at[stage, o if arrive is None else arrive], device_id=dev,
            device_id_type=pl.DeviceIdType.MESH,
        )

    smalls = [
        pltpu.make_async_copy(src, dst, small_sem.at[k])
        for k, (src, dst) in enumerate(
            (
                (momenta_hbm, momenta), (tindex_hbm, tindex), (tweight_hbm, tweight),
                (lengths_hbm, lengths), (chan_hbm, chan),
            )
        )
    ]
    for c in smalls:
        c.start()
    start_loads(s_hbm, buf, load_sem, (0,))
    barrier = pltpu.get_barrier_semaphore()

    def greet(dev):
        pl.semaphore_signal(barrier, inc=1, device_id=dev, device_id_type=pl.DeviceIdType.MESH)

    alone = b == y
    for o in FAR:
        greet(y_dev(step(y, o)))
    for o in FAR:
        greet(z_dev(step(z, o)))
    for o in range(1, 8):
        greet(b_dev(step(b, o), y))
        greet(b_dev(y, step(y, o)))

    @pl.when(jnp.logical_not(alone))
    def _():
        greet(b_dev(y, y))

    start_loads(s_hbm, buf, load_sem, (1, 2))
    fill_phases(rhs, tab)
    rows = lax.broadcasted_iota(jnp.int32, (8, 128), 0)
    lanes = lax.broadcasted_iota(jnp.int32, (8, 128), 1)
    for c in smalls:
        c.wait()
    for g in range(8):
        for k in range(4):
            n = chan[k % 2, 2 * g + k // 2]
            spots[4 * g + k] = 40 * (n // 16) + n % 16
    mom_box[0] = jnp.zeros((8, 128), jnp.float32)
    mom_box[0, 0:3, 0:16] = momenta[...].astype(jnp.float32)
    mom_box[0] = pltpu.roll(mom_box[0], 16 * y, 1)
    term_box[0] = jnp.zeros((8, 128), jnp.float32)
    live = lax.broadcasted_iota(jnp.int32, (2, 24), 1) + (8 * z + b) * 24
    owner = lax.broadcasted_iota(jnp.int32, (2, 24), 0)
    size = jnp.where(owner == 0, lengths[0], lengths[1])
    for side in range(2):
        slot, lane = place(tindex[side].astype(jnp.float32))
        term_box[0, 2 * side : 2 * side + 2, 0:24] = slot * 128.0 + lane
    term_box[0, 4:6, 0:24] = jnp.where(live < size, tweight[...], 0.0)
    term_box[0] = pltpu.roll(term_box[0], 32 * lax.rem(b, 4), 1)
    blocks(0, y, buf, load_sem, wide, skp, lhs, rhs, acc)

    pl.semaphore_wait(barrier, jnp.where(alone, 28, 29))
    sent = []
    for o in range(1, 8):
        c = copy(mom_box.at[0], mom_box.at[o], 0, o, y_dev(step(y, o)))
        c.start()
        sent.append(c)
    boxes = []
    for o in range(1, 8):
        c = copy(term_box.at[0], term_box.at[o], 1, o, b_dev(step(b, o), y))
        c.start()
        boxes.append(c)


    blocks(1, y, buf, load_sem, wide, skp, lhs, rhs, acc)
    blocks(2, y, buf, load_sem, wide, skp, lhs, rhs, acc)
    acc[...] += jnp.dot(lhs[:, 1024:], rhs[1024:, :], preferred_element_type=jnp.float32)
    for c in sent[:7]:
        c.wait_recv()
    mom = mom_box[0]
    for o in range(1, 8):
        mom = mom + mom_box[o]
    finish(mom, 4 * sx, 16 * x, SCALE, spots, acc, zbuf, part1)

    hops = []
    for o in range(1, 8):
        g = step(b, o)
        c = copy(
            part1.at[pl.ds(pl.multiple_of(40 * g, 8), 40)], got1.at[o], 3, o, b_dev(g, y)
        )
        c.start()
        hops.append(c)
    for c in boxes:
        c.wait_recv()
    for half in range(2):
        joined = jnp.zeros((8, 128), jnp.float32)
        for o in range(8):
            source = lax.rem(b + 8 - o, 8)
            joined = joined + jnp.where(source // 4 == half, term_box[o], 0.0)
        term_all[z, half] = joined
    sent += boxes
    boxes = []
    for o in range(1, 8):
        c = copy(term_all.at[z], term_all.at[z], 2, o, z_dev(step(z, o)))
        c.start()
        boxes.append(c)
    slot, inner, k, kind = locate((lanes + 54 * (8 * lax.rem(z, 4) + rows)).astype(jnp.float32))
    mine = (slot == y.astype(jnp.float32)) & (lanes < 54)
    held = [
        jnp.max(jnp.where(mine & (kind == v), inner, 0.0), axis=1, keepdims=True) for v in range(2)
    ]
    within = lax.rem(lanes, 32)
    second = within >= 12
    cols[0] = jnp.where(second, held[1], held[0]) * 12.0 + jnp.where(
        second, within - 12, within
    ).astype(jnp.float32)
    cols[1] = slot
    cols[2] = 12.0 * kind + k
    total = part1[pl.ds(pl.multiple_of(40 * b, 8), 40), :]
    for c in hops:
        c.wait_recv()
    for o in range(1, 8):
        total = total + got1[o]
    sum1[...] = total
    sent += hops

    hops = []
    for o in range(1, 8):
        g = step(z, o)
        c = copy(
            sum1.at[pl.ds(pl.multiple_of(16 * (g // 4), 8), 24)], got2.at[o], 4, o, z_dev(g)
        )
        c.start()
        hops.append(c)
    low = z < 4
    total = jnp.where(low, sum1[0:24], sum1[16:40])
    for c in hops:
        c.wait_recv()
    for o in range(1, 8):
        total = total + got2[o]
    sent += hops
    table = jnp.where(low, total[0:16], total[8:24])
    rest = jnp.where(low, total[16:24], total[0:8])
    for g in range(8):
        lane = jnp.broadcast_to(cols[0, g : g + 1], (8, 128)).astype(jnp.int32)
        packed = []
        for u in range(2):
            have = pick(table[8 * u : 8 * u + 8], lane)
            packed.append(jnp.where(lax.rem(lanes // 32, 2) == 1, pltpu.roll(have, 4, 0), have))
        part3[g, 0:8] = rest
        part3[g, 8:12] = jnp.where(lanes < 64, packed[0], packed[1])[0:4]

    def third(o, arrive):
        g = step(b, o)
        return copy(part3.at[g], got3.at[arrive], 5, o, b_dev(g, b), arrive)

    for o in range(1, 8):
        third(o, y).start()

    @pl.when(jnp.logical_not(alone))
    def _():
        third(0, y).start()

    @pl.when(alone)
    def _():
        got3[y] = part3[y]

    for c in boxes:
        c.wait_recv()
    sent += boxes
    terms = [term_all[:, :, k, :].reshape(16, 128) for k in range(6)]
    places = []
    for k in range(4):
        slot = jnp.floor((terms[k] + 0.5) * (1.0 / 128.0))
        places.append((slot, (terms[k] - 128.0 * slot).astype(jnp.int32)))

    for k in range(8):
        @pl.when(jnp.logical_not(alone & (y == k)))
        def _():
            third(0, k).wait_recv()

    slot = jnp.broadcast_to(cols[1, pl.ds(b, 1), :], (8, 128))
    lane = jnp.broadcast_to(cols[2, pl.ds(b, 1), :], (8, 128)).astype(jnp.int32)
    quads = [jnp.zeros((8, 128), jnp.float32) for g in range(4)]
    for v in range(4):
        have = jnp.concatenate([got3[2 * v, 8:12], got3[2 * v + 1, 8:12]], axis=0)
        here = slot == jnp.where(rows < 4, 2.0 * v, 2.0 * v + 1.0)
        for g in range(4):
            quads[g] = jnp.where(here, pick(have, lane + 32 * g), quads[g])
    for g in range(4):
        whole = quads[g] + pltpu.roll(quads[g], 4, 0)
        out[4 * g : 4 * g + 4, :] = whole[0:4, :54]

    answer = jnp.zeros((2, 2), jnp.float32)
    at_row = lax.broadcasted_iota(jnp.int32, (2, 2), 0)
    at_col = lax.broadcasted_iota(jnp.int32, (2, 2), 1)
    for h in range(2):
        sides = []
        for side in range(2):
            slot, lane = places[2 * side + h]
            both = []
            for part in range(2):
                row = 4 * h + 2 * side + part
                chosen = []
                for u in range(2):
                    value = jnp.zeros((8, 128), jnp.float32)
                    for k in range(8):
                        have = jnp.broadcast_to(got3[k, row : row + 1], (8, 128))
                        have = pick(have, lane[8 * u : 8 * u + 8])
                        value = jnp.where(slot[8 * u : 8 * u + 8] == k, have, value)
                    chosen.append(value)
                both.append(jnp.concatenate(chosen, axis=0))
            sides.append(tuple(both))
        prod = cmul(sides[0], sides[1])
        for part in range(2):
            answer = jnp.where(
                (at_row == part) & (at_col == h), jnp.sum(terms[4 + h] * prod[part]), answer
            )
    corr[...] = answer

    for c in sent:
        c.wait_send()
    for o in range(1, 8):
        third(o, y).wait_send()

    @pl.when(jnp.logical_not(alone))
    def _():
        third(0, y).wait_send()


def hand_over(block, value, out, corr, sem):
    copies = [
        pltpu.make_async_copy(block, out, sem.at[0]),
        pltpu.make_async_copy(value, corr, sem.at[1]),
    ]
    for c in copies:
        c.start()
    for c in copies:
        c.wait()


def local(propagator, momenta, chan_moms, term_index, term_weight, lengths):
    f32, i32 = jnp.float32, jnp.int32
    vmem = pl.BlockSpec(memory_space=pltpu.VMEM)
    results = pl.pallas_call(
        kernel,
        out_shape=(
            pltpu.VMEM((16, 54), f32),
            pltpu.VMEM((2, 2), f32),
        ),
        in_specs=[pl.BlockSpec(memory_space=pl.ANY)] * 6,
        out_specs=(vmem, vmem),
        scratch_shapes=[
            pltpu.VMEM((2, 12, 12, 12, 4, 128), jnp.bfloat16),
            pltpu.VMEM((2, 12, 12, 16, 128), f32),
            pltpu.VMEM((1536, 256), jnp.bfloat16),
            pltpu.VMEM((2, 16, 128), f32),
            pltpu.VMEM((4, 3, 3, 6, 8, 128), f32),
            pltpu.VMEM((96 * PAIRS, 1536), jnp.bfloat16),
            pltpu.VMEM((96 * PAIRS, 256), f32),
            pltpu.VMEM((2, 512, 128), f32),
            pltpu.VMEM((3, 16), i32),
            pltpu.SMEM((2, 16), i32),
            pltpu.SMEM((32,), i32),
            pltpu.VMEM((2, 2, 24), i32),
            pltpu.VMEM((2, 24), f32),
            pltpu.SMEM((2,), i32),
            pltpu.VMEM((8, 8, 128), f32),
            pltpu.VMEM((8, 8, 128), f32),
            pltpu.VMEM((8, 2, 8, 128), f32),
            pltpu.VMEM((320, 128), f32),
            pltpu.VMEM((8, 40, 128), f32),
            pltpu.VMEM((40, 128), f32),
            pltpu.VMEM((8, 24, 128), f32),
            pltpu.VMEM((8, 12, 128), f32),
            pltpu.VMEM((8, 12, 128), f32),
            pltpu.VMEM((3, 8, 128), f32),
            pltpu.SemaphoreType.DMA((3,)),
            pltpu.SemaphoreType.DMA((5,)),
            pltpu.SemaphoreType.DMA((6, 8)),
            pltpu.SemaphoreType.DMA((6, 8)),
        ],
        compiler_params=pltpu.CompilerParams(
            collective_id=0, has_side_effects=True, vmem_limit_bytes=62 * 2**20
        ),
    )(propagator, momenta.T, chan_moms.T, term_index, term_weight, lengths)
    return pl.pallas_call(
        hand_over,
        out_shape=(
            jax.ShapeDtypeStruct((16, 54), f32),
            jax.ShapeDtypeStruct((2, 2), f32),
        ),
        in_specs=[vmem] * 2,
        out_specs=[pl.BlockSpec(memory_space=pl.ANY)] * 2,
        scratch_shapes=[pltpu.SemaphoreType.DMA((2,))],
        compiler_params=pltpu.CompilerParams(vmem_limit_bytes=2**20),
    )(*results)


def solution(mesh):
    in_specs = (
        P(None, None, None, "sx", "sy"),
        P("mom", None),
        P(),
        P(None, "mom", ("sx", "sy")),
        P("mom", ("sx", "sy")),
        P("mom"),
    )
    out_specs = (P("mom", ("sx", "sy")), P(None, "mom"))
    return jax.shard_map(local, mesh=mesh, in_specs=in_specs, out_specs=out_specs, check_vma=False)
```

```python
import math
import jax
import jax.numpy as jnp
from jax import lax
from jax.experimental import pallas as pl
from jax.experimental.pallas import tpu as pltpu
from jax.sharding import PartitionSpec as P

LAT = 96
PAIRS = 10
SCALE = 1.0 / math.sqrt(393216)
IM = 24
FAR = (4, 3, 5, 2, 6, 1, 7)
COLOURS = ((1, 2, 0), (2, 0, 1), (0, 1, 2))


def sine(turns):
    u = turns - 96.0 * jnp.floor(turns * (1.0 / 96.0) + 0.5)
    v = jnp.where(u > 24.0, 48.0 - u, jnp.where(u < -24.0, -48.0 - u, u))
    x = v * (2.0 * math.pi / 96.0)
    y = x * x
    r = jnp.float32(1.0 / 6227020800.0)
    for c in (-1.0 / 39916800.0, 1.0 / 362880.0, -1.0 / 5040.0, 1.0 / 120.0, -1.0 / 6.0, 1.0):
        r = r * y + c
    return x * r


def cosine(turns):
    return sine(turns + 24.0)


def cmul(a, b):
    return (a[0] * b[0] - a[1] * b[1], a[0] * b[1] + a[1] * b[0])


def cadd(a, b):
    return (a[0] + b[0], a[1] + b[1])


def csub(a, b):
    return (a[0] - b[0], a[1] - b[1])


def start_loads(s_hbm, buf, sem, thirds):
    for t in thirds:
        for c in range(4 * t, 4 * t + 4):
            pltpu.make_async_copy(
                s_hbm.at[:, :, :, :, pl.ds(128 * c, 128)], buf.at[:, :, :, c], sem.at[t]
            ).start()


def wait_load(buf, sem, t):
    part = buf.at[:, :, :, pl.ds(4 * t, 4)]
    pltpu.make_async_copy(part, part, sem.at[t]).wait()


def fill_phases(rhs, tab):
    lane = lax.broadcasted_iota(jnp.int32, (1, 128), 1).astype(jnp.float32)
    p2 = jnp.floor((lane + 0.5) * (1.0 / 9.0))
    p3 = lane - 9.0 * p2 - 4.0
    p2 = p2 - 4.0
    x3 = lax.broadcasted_iota(jnp.int32, (96, 128), 0).astype(jnp.float32)
    c3 = cosine(p3 * x3)
    s3 = sine(p3 * x3)
    x2 = lax.broadcasted_iota(jnp.int32, (16, 128), 0).astype(jnp.float32)
    tab[0] = cosine(p2 * x2)
    tab[1] = sine(p2 * x2)

    def row(b, _):
        c2 = tab[0, pl.ds(b, 1), :]
        s2 = tab[1, pl.ds(b, 1), :]
        at = pl.ds(pl.multiple_of(96 * b, 96), 96)
        rhs[at, 0:128] = (c2 * c3 - s2 * s3).astype(jnp.bfloat16)
        rhs[at, 128:256] = (s2 * c3 + c2 * s3).astype(jnp.bfloat16)
        return 0

    lax.fori_loop(0, 16, row, 0)


def blocks(t, y, buf, sem, wide, skp, lhs, rhs, acc):
    low = lax.broadcasted_iota(jnp.int32, (8, 128), 0) < 4

    def rot(v):
        return pltpu.roll(v, 4, 0)

    def widen(i, _):
        for part in range(2):
            for row in range(12):
                wide[part, row, i] = (
                    buf[part, row, i, pl.ds(4 * t, 4)].reshape(16, 128).astype(jnp.float32)
                )
        return 0

    def load(part, row, i, h):
        return wide[part, row, i, 8 * h : 8 * h + 8]

    def pack_k(kp, _):
        for c in range(3):
            made = []
            for part in range(2):
                four = []
                for h in range(2):
                    ah = load(part, 4 * c, 2 * kp, h)
                    bh = load(part, 4 * c, 2 * kp + 1, h)
                    four.append(jnp.where(low, ah, rot(bh)))
                    four.append(jnp.where(low, rot(ah), bh))
                made.append(four)
            for ch in range(4):
                re, im = made[0][ch], made[1][ch]
                skp[ch, 0, c, kp] = re
                skp[ch, 1, c, kp] = im
                skp[ch, 2, c, kp] = re + im
        return 0

    def spins(idx, h):
        return [
            [(load(0, 4 * a + s, idx, h), load(1, 4 * a + s, idx, h)) for s in range(4)]
            for a in range(3)
        ]

    def pair(p, _):
        e = PAIRS * y + p
        d = e // 12
        i = e - 12 * d
        j = lax.rem(i + d, 12)
        for h in range(2):
            xh, yh = spins(i, h), spins(j, h)
            q = {}
            for a, b, c in COLOURS:
                total = None
                for s, u in ((0, 1), (2, 3)):
                    term = csub(cmul(xh[a][s], yh[b][u]), cmul(xh[a][u], yh[b][s]))
                    more = csub(cmul(yh[a][s], xh[b][u]), cmul(yh[a][u], xh[b][s]))
                    term = cadd(term, more)
                    total = term if total is None else cadd(total, term)
                re, im = total
                q[c] = (re, im)
            for odd in range(2):
                ch = 2 * h + odd
                dup = {}
                for c in range(3):
                    both = []
                    for v in q[c]:
                        r = rot(v)
                        both.append(jnp.where(low, r, v) if odd else jnp.where(low, v, r))
                    dup[c] = both + [both[0] + both[1]]
                for kq in range(3):
                    halves = []
                    for kp in (2 * kq, 2 * kq + 1):
                        tot = []
                        for part in range(3):
                            tot.append(
                                dup[0][part] * skp[ch, part, 0, kp]
                                + dup[1][part] * skp[ch, part, 1, kp]
                                + dup[2][part] * skp[ch, part, 2, kp]
                            )
                        halves.append((tot[0] - tot[1], tot[2] - tot[0] - tot[1]))
                    for part in range(2):
                        rows = pl.ds(pl.multiple_of(96 * p + 48 * part + 16 * kq, 16), 16)
                        lanes = pl.ds(pl.multiple_of(512 * t + 128 * ch, 128), 128)
                        lhs[rows, lanes] = jnp.concatenate(
                            [halves[0][part], halves[1][part]], axis=0
                        ).astype(jnp.bfloat16)
        return 0

    wait_load(buf, sem, t)
    lax.fori_loop(0, 12, widen, 0)
    lax.fori_loop(0, 6, pack_k, 0)
    def two(p, _):
        if t:
            rows = pl.ds(pl.multiple_of(192 * p, 64), 192)
            depth = slice(512 * t - 512, 512 * t)
            prod = jnp.dot(lhs[rows, depth], rhs[depth, :], preferred_element_type=jnp.float32)
            acc[rows, :] = prod if t == 1 else acc[rows, :] + prod
        pair(2 * p, 0)
        pair(2 * p + 1, 0)
        return 0

    lax.fori_loop(0, PAIRS // 2, two, 0)


def pick(x, lane):
    return jnp.take_along_axis(x, lane, axis=1, mode="promise_in_bounds")


def finish(mom, x0, y0, scale, spots, acc, zbuf, part1):
    x1 = lax.broadcasted_iota(jnp.int32, (8, 128), 0) % 4 + x0
    turns = mom[0:1] * x1.astype(jnp.float32) + mom[1:2] * y0.astype(jnp.float32)
    fc, fs = cosine(turns) * scale, sine(turns) * scale
    cell = (9.0 * mom[1:2] + mom[2:3] + 40.0).astype(jnp.int32)
    cell = jnp.broadcast_to(cell, (8, 128))

    def pair(p, _):
        for g in range(6):
            r = acc[pl.ds(pl.multiple_of(96 * p + 8 * g, 8), 8), :]
            m = acc[pl.ds(pl.multiple_of(96 * p + 48 + 8 * g, 8), 8), :]
            re = pick(r[:, :128] + m[:, 128:], cell)
            im = pick(m[:, :128] - r[:, 128:], cell)
            at = pl.ds(pl.multiple_of(48 * p + 8 * g, 8), 8)
            zbuf[0, at, :] = fc * re + fs * im
            zbuf[1, at, :] = fc * im - fs * re
        return 0

    lax.fori_loop(0, PAIRS, pair, 0)
    zbuf[:, 480:512, :] = jnp.zeros((2, 32, 128), jnp.float32)
    for part in range(2):
        tot = zbuf[part, pl.ds(0, 128, stride=4), :]
        for k in range(1, 4):
            tot = tot + zbuf[part, pl.ds(k, 128, stride=4), :]
        turned = tot.T
        for g in range(8):
            part1[40 * g + IM * part : 40 * g + IM * part + 16, :] = turned[16 * g : 16 * g + 16]
    for g in range(8):
        for k in range(4):
            row = spots[4 * g + k]
            for part in range(2):
                at = 40 * g + 16 + 2 * k + part
                part1[at : at + 1, :] = part1[pl.ds(row + IM * part, 1), :]


def locate(m):
    i = jnp.floor((m + 0.5) * (1.0 / 144.0))
    r = m - 144.0 * i
    j = jnp.floor((r + 0.5) * (1.0 / 12.0))
    k = r - 12.0 * j
    d = j - i
    d = jnp.where(d < 0.0, d + 12.0, d)
    flip = (d > 6.0) | ((d == 6.0) & (i >= 6.0))
    e = jnp.where(flip, 12.0 * (12.0 - d) + j, 12.0 * d + i)
    slot = jnp.floor((e + 0.5) * (1.0 / PAIRS))
    odd = i - 2.0 * jnp.floor(0.5 * i)
    kind = jnp.where(flip, 1.0 - odd, odd)
    return slot, e - PAIRS * slot, k, kind


def place(m):
    slot, inner, k, _ = locate(m)
    return slot, inner * 12.0 + k


def kernel(
    s_hbm, momenta_hbm, chan_hbm, tindex_hbm, tweight_hbm, lengths_hbm, out, corr,
    buf, wide, rhs, tab, skp, lhs, acc, zbuf, momenta, chan, spots, tindex, tweight, lengths,
    mom_box, term_box, term_all, part1, got1, sum1, got2, part3, got3, cols,
    load_sem, small_sem, send_sem, recv_sem,
):
    sx, x, y = lax.axis_index("sx"), lax.axis_index("sy"), lax.axis_index("mom")
    z, core = sx // 2, lax.rem(sx, 2)
    b = 4 * core + x

    def b_dev(g, plane):
        return (2 * z + g // 4, lax.rem(g, 4), plane)

    def z_dev(g):
        return (2 * g + core, x, y)

    def y_dev(g):
        return (sx, x, g)

    def step(v, o):
        return lax.rem(v + o, 8)

    def copy(src, dst, stage, o, dev, arrive=None):
        return pltpu.make_async_remote_copy(
            src_ref=src, dst_ref=dst, send_sem=send_sem.at[stage, o],
            recv_sem=recv_sem.at[stage, o if arrive is None else arrive], device_id=dev,
            device_id_type=pl.DeviceIdType.MESH,
        )

    smalls = [
        pltpu.make_async_copy(src, dst, small_sem.at[k])
        for k, (src, dst) in enumerate(
            (
                (momenta_hbm, momenta), (tindex_hbm, tindex), (tweight_hbm, tweight),
                (lengths_hbm, lengths), (chan_hbm, chan),
            )
        )
    ]
    for c in smalls:
        c.start()
    start_loads(s_hbm, buf, load_sem, (0,))
    barrier = pltpu.get_barrier_semaphore()

    def greet(dev):
        pl.semaphore_signal(barrier, inc=1, device_id=dev, device_id_type=pl.DeviceIdType.MESH)

    alone = b == y
    for o in FAR:
        greet(y_dev(step(y, o)))
    for o in FAR:
        greet(z_dev(step(z, o)))
    for o in range(1, 8):
        greet(b_dev(step(b, o), y))
        greet(b_dev(y, step(y, o)))

    @pl.when(jnp.logical_not(alone))
    def _():
        greet(b_dev(y, y))

    start_loads(s_hbm, buf, load_sem, (1, 2))
    fill_phases(rhs, tab)
    rows = lax.broadcasted_iota(jnp.int32, (8, 128), 0)
    lanes = lax.broadcasted_iota(jnp.int32, (8, 128), 1)
    for c in smalls:
        c.wait()
    for g in range(8):
        for k in range(4):
            n = chan[k % 2, 2 * g + k // 2]
            spots[4 * g + k] = 40 * (n // 16) + n % 16
    mom_box[0] = jnp.zeros((8, 128), jnp.float32)
    mom_box[0, 0:3, 0:16] = momenta[...].astype(jnp.float32)
    mom_box[0] = pltpu.roll(mom_box[0], 16 * y, 1)
    term_box[0] = jnp.zeros((8, 128), jnp.float32)
    live = lax.broadcasted_iota(jnp.int32, (2, 24), 1) + (8 * z + b) * 24
    owner = lax.broadcasted_iota(jnp.int32, (2, 24), 0)
    size = jnp.where(owner == 0, lengths[0], lengths[1])
    for side in range(2):
        slot, lane = place(tindex[side].astype(jnp.float32))
        term_box[0, 2 * side : 2 * side + 2, 0:24] = slot * 128.0 + lane
    term_box[0, 4:6, 0:24] = jnp.where(live < size, tweight[...], 0.0)
    term_box[0] = pltpu.roll(term_box[0], 32 * lax.rem(b, 4), 1)
    blocks(0, y, buf, load_sem, wide, skp, lhs, rhs, acc)

    pl.semaphore_wait(barrier, jnp.where(alone, 28, 29))
    sent = []
    for o in FAR:
        c = copy(mom_box.at[0], mom_box.at[o], 0, o, y_dev(step(y, o)))
        c.start()
        sent.append(c)
    boxes = []
    for o in range(1, 8):
        c = copy(term_box.at[0], term_box.at[o], 1, o, b_dev(step(b, o), y))
        c.start()
        boxes.append(c)


    blocks(1, y, buf, load_sem, wide, skp, lhs, rhs, acc)
    blocks(2, y, buf, load_sem, wide, skp, lhs, rhs, acc)
    acc[...] += jnp.dot(lhs[:, 1024:], rhs[1024:, :], preferred_element_type=jnp.float32)
    for c in sent[:7]:
        c.wait_recv()
    mom = mom_box[0]
    for o in range(1, 8):
        mom = mom + mom_box[o]
    finish(mom, 4 * sx, 16 * x, SCALE, spots, acc, zbuf, part1)

    hops = []
    for o in range(1, 8):
        g = step(b, o)
        c = copy(
            part1.at[pl.ds(pl.multiple_of(40 * g, 8), 40)], got1.at[o], 3, o, b_dev(g, y)
        )
        c.start()
        hops.append(c)
    for c in boxes:
        c.wait_recv()
    for half in range(2):
        joined = jnp.zeros((8, 128), jnp.float32)
        for o in range(8):
            source = lax.rem(b + 8 - o, 8)
            joined = joined + jnp.where(source // 4 == half, term_box[o], 0.0)
        term_all[z, half] = joined[0:6]
    sent += boxes
    boxes = []
    for o in range(1, 8):
        c = copy(term_all.at[z], term_all.at[z], 2, o, z_dev(step(z, o)))
        c.start()
        boxes.append(c)
    slot, inner, k, kind = locate((lanes + 54 * (8 * lax.rem(z, 4) + rows)).astype(jnp.float32))
    mine = (slot == y.astype(jnp.float32)) & (lanes < 54)
    held = [
        jnp.max(jnp.where(mine & (kind == v), inner, 0.0), axis=1, keepdims=True) for v in range(2)
    ]
    within = lax.rem(lanes, 32)
    second = within >= 12
    cols[0] = jnp.where(second, held[1], held[0]) * 12.0 + jnp.where(
        second, within - 12, within
    ).astype(jnp.float32)
    cols[1] = slot
    cols[2] = 12.0 * kind + k
    total = part1[pl.ds(pl.multiple_of(40 * b, 8), 40), :]
    for c in hops:
        c.wait_recv()
    for o in range(1, 8):
        total = total + got1[o]
    sum1[...] = total
    sent += hops

    hops = []
    for o in range(1, 8):
        g = step(z, o)
        c = copy(
            sum1.at[pl.ds(pl.multiple_of(16 * (g // 4), 8), 24)], got2.at[o], 4, o, z_dev(g)
        )
        c.start()
        hops.append(c)
    low = z < 4
    total = jnp.where(low, sum1[0:24], sum1[16:40])
    for c in hops:
        c.wait_recv()
    for o in range(1, 8):
        total = total + got2[o]
    sent += hops
    table = jnp.where(low, total[0:16], total[8:24])
    rest = jnp.where(low, total[16:24], total[0:8])
    for g in range(8):
        lane = jnp.broadcast_to(cols[0, g : g + 1], (8, 128)).astype(jnp.int32)
        packed = []
        for u in range(2):
            have = pick(table[8 * u : 8 * u + 8], lane)
            packed.append(jnp.where(lax.rem(lanes // 32, 2) == 1, pltpu.roll(have, 4, 0), have))
        part3[g, 0:8] = rest
        part3[g, 8:12] = jnp.where(lanes < 64, packed[0], packed[1])[0:4]

    def third(o, arrive):
        g = step(b, o)
        return copy(part3.at[g], got3.at[arrive], 5, o, b_dev(g, b), arrive)

    for o in range(1, 8):
        third(o, y).start()

    @pl.when(jnp.logical_not(alone))
    def _():
        third(0, y).start()

    @pl.when(alone)
    def _():
        got3[y] = part3[y]

    for c in boxes:
        c.wait_recv()
    sent += boxes
    terms = [term_all[:, :, k, :].reshape(16, 128) for k in range(6)]
    places = []
    for k in range(4):
        slot = jnp.floor((terms[k] + 0.5) * (1.0 / 128.0))
        places.append((slot, (terms[k] - 128.0 * slot).astype(jnp.int32)))

    for k in range(8):
        @pl.when(jnp.logical_not(alone & (y == k)))
        def _():
            third(0, k).wait_recv()

    slot = jnp.broadcast_to(cols[1, pl.ds(b, 1), :], (8, 128))
    lane = jnp.broadcast_to(cols[2, pl.ds(b, 1), :], (8, 128)).astype(jnp.int32)
    quads = [jnp.zeros((8, 128), jnp.float32) for g in range(4)]
    for v in range(4):
        have = jnp.concatenate([got3[2 * v, 8:12], got3[2 * v + 1, 8:12]], axis=0)
        here = slot == jnp.where(rows < 4, 2.0 * v, 2.0 * v + 1.0)
        for g in range(4):
            quads[g] = jnp.where(here, pick(have, lane + 32 * g), quads[g])
    for g in range(4):
        whole = quads[g] + pltpu.roll(quads[g], 4, 0)
        out[4 * g : 4 * g + 4, :] = whole[0:4, :54]

    answer = jnp.zeros((2, 2), jnp.float32)
    at_row = lax.broadcasted_iota(jnp.int32, (2, 2), 0)
    at_col = lax.broadcasted_iota(jnp.int32, (2, 2), 1)
    for h in range(2):
        sides = []
        for side in range(2):
            slot, lane = places[2 * side + h]
            both = []
            for part in range(2):
                row = 4 * h + 2 * side + part
                chosen = []
                for u in range(2):
                    value = jnp.zeros((8, 128), jnp.float32)
                    for k in range(8):
                        have = jnp.broadcast_to(got3[k, row : row + 1], (8, 128))
                        have = pick(have, lane[8 * u : 8 * u + 8])
                        value = jnp.where(slot[8 * u : 8 * u + 8] == k, have, value)
                    chosen.append(value)
                both.append(jnp.concatenate(chosen, axis=0))
            sides.append(tuple(both))
        prod = cmul(sides[0], sides[1])
        for part in range(2):
            answer = jnp.where(
                (at_row == part) & (at_col == h), jnp.sum(terms[4 + h] * prod[part]), answer
            )
    corr[...] = answer

    for c in sent:
        c.wait_send()
    for o in range(1, 8):
        third(o, y).wait_send()

    @pl.when(jnp.logical_not(alone))
    def _():
        third(0, y).wait_send()


def hand_over(block, value, out, corr, sem):
    copies = [
        pltpu.make_async_copy(block, out, sem.at[0]),
        pltpu.make_async_copy(value, corr, sem.at[1]),
    ]
    for c in copies:
        c.start()
    for c in copies:
        c.wait()


def local(propagator, momenta, chan_moms, term_index, term_weight, lengths):
    f32, i32 = jnp.float32, jnp.int32
    vmem = pl.BlockSpec(memory_space=pltpu.VMEM)
    results = pl.pallas_call(
        kernel,
        out_shape=(
            pltpu.VMEM((16, 54), f32),
            pltpu.VMEM((2, 2), f32),
        ),
        in_specs=[pl.BlockSpec(memory_space=pl.ANY)] * 6,
        out_specs=(vmem, vmem),
        scratch_shapes=[
            pltpu.VMEM((2, 12, 12, 12, 4, 128), jnp.bfloat16),
            pltpu.VMEM((2, 12, 12, 16, 128), f32),
            pltpu.VMEM((1536, 256), jnp.bfloat16),
            pltpu.VMEM((2, 16, 128), f32),
            pltpu.VMEM((4, 3, 3, 6, 8, 128), f32),
            pltpu.VMEM((96 * PAIRS, 1536), jnp.bfloat16),
            pltpu.VMEM((96 * PAIRS, 256), f32),
            pltpu.VMEM((2, 512, 128), f32),
            pltpu.VMEM((3, 16), i32),
            pltpu.SMEM((2, 16), i32),
            pltpu.SMEM((32,), i32),
            pltpu.VMEM((2, 2, 24), i32),
            pltpu.VMEM((2, 24), f32),
            pltpu.SMEM((2,), i32),
            pltpu.VMEM((8, 8, 128), f32),
            pltpu.VMEM((8, 8, 128), f32),
            pltpu.VMEM((8, 2, 6, 128), f32),
            pltpu.VMEM((320, 128), f32),
            pltpu.VMEM((8, 40, 128), f32),
            pltpu.VMEM((40, 128), f32),
            pltpu.VMEM((8, 24, 128), f32),
            pltpu.VMEM((8, 12, 128), f32),
            pltpu.VMEM((8, 12, 128), f32),
            pltpu.VMEM((3, 8, 128), f32),
            pltpu.SemaphoreType.DMA((3,)),
            pltpu.SemaphoreType.DMA((5,)),
            pltpu.SemaphoreType.DMA((6, 8)),
            pltpu.SemaphoreType.DMA((6, 8)),
        ],
        compiler_params=pltpu.CompilerParams(
            collective_id=0, has_side_effects=True, vmem_limit_bytes=62 * 2**20
        ),
    )(propagator, momenta.T, chan_moms.T, term_index, term_weight, lengths)
    return pl.pallas_call(
        hand_over,
        out_shape=(
            jax.ShapeDtypeStruct((16, 54), f32),
            jax.ShapeDtypeStruct((2, 2), f32),
        ),
        in_specs=[vmem] * 2,
        out_specs=[pl.BlockSpec(memory_space=pl.ANY)] * 2,
        scratch_shapes=[pltpu.SemaphoreType.DMA((2,))],
        compiler_params=pltpu.CompilerParams(vmem_limit_bytes=2**20),
    )(*results)


def solution(mesh):
    in_specs = (
        P(None, None, None, "sx", "sy"),
        P("mom", None),
        P(),
        P(None, "mom", ("sx", "sy")),
        P("mom", ("sx", "sy")),
        P("mom"),
    )
    out_specs = (P("mom", ("sx", "sy")), P(None, "mom"))
    return jax.shard_map(local, mesh=mesh, in_specs=in_specs, out_specs=out_specs, check_vma=False)
```
